32 devices in a mesh: replica: 2 (over y), ep: 8 (over z, x), tp: 2 (over core).
Axes of the slice: x: 2, y: 2, z: 4, core: 2. Of those that a mesh axis runs over, the one named last changes fastest.
Arguments:
- residual_in: bfloat16 [1024, 3584], P(('replica', 'ep')), parts along dimension 0, may hold values from -6 to 6
- dense_terms: bfloat16 [2, 1024, 3584], P('tp', ('replica', 'ep')), parts along dimension 1, may hold values from -6 to 6
- norm_gain: float32 [3584], replicated, may hold values from 0.1 to 1.9
- router_weight: bfloat16 [3584, 64], P('tp'), may hold values from -0.09375 to 0.09375
- routes: int32 [1024, 8], P(('replica', 'ep')), parts along dimension 0, may hold values from 0 to 63, all different within a row; in each aligned block of 64 rows (0 to 63, 64 to 127, ...) at most 12 rows name the same one
- placement: int32 [64], replicated, may hold values from 0 to 63, each once
- up_weight: bfloat16 [3584, 65536], P('tp', 'ep'), may hold values from -0.09375 to 0.09375
- down_weight: bfloat16 [65536, 3584], P('ep', 'tp'), may hold values from -0.1875 to 0.1875
Outputs:
- mixed: bfloat16 [1024, 3584], P(('replica', 'ep'), 'tp'), parts along dimension 0
The draws below stay inside these ranges and needn't reach their ends.
There are 2 independent parts, one for each index of `replica`. The reference program is written for one: setup_inputs(seed, part) draws one part's arguments, and reference() takes and returns one part's arrays. A program takes and returns all parts, laid end to end along the dimension named above; an argument that names none is the same for every part. Nothing has to cross between parts.
Inputs may be any that keep to these rules, and one draw needn't show every extreme that they name: `routes`: in the rows of one index of ep no expert is named by more than 12 rows. `placement`: each slot holds exactly one expert.
All inputs are finite; a program needn't handle non-finite values.
Results may differ from the reference program's by a relative error of at most 0.011.
Values may be sent and summed in bfloat16 or wider, within the bound.
A program may use at most 256 MiB of HBM per device.

```python
import math
import jax
import jax.numpy as jnp
import numpy as np
from jax import lax

D = 3584
FF_E = 1024
EXPERTS = 64
TOPK = 8
TOK_DEV = 64
TOKENS = 512
CAP = 12
COLS_DEV = 8192
ROWS = 512
N_EP = 8
N_TP = 2


def block_levels(stream_key, dims, pieces, low, high):
    factor_of = 1.0
    for position, blocks in pieces:
        draws = jax.random.uniform(jax.random.fold_in(jax.random.fold_in(stream_key, 6), position), (blocks,), jnp.float32, low / len(pieces), high / len(pieces))
        factor_of = factor_of * jnp.repeat(jnp.exp(draws), dims[position] // blocks).reshape((-1,) + (1,) * (len(dims) - 1 - position))
    return factor_of


def shared_out(stream_key, own, number, rows, amount, top, bound, slope):
    sequence = jax.random.permutation(stream_key, amount)
    crowded, common = shares(amount, rows * top, bound, slope, True), shares(amount, rows * top, bound, slope, False)
    places = jnp.arange(amount)

    def named(tallies, turn):
        used = int((tallies > 0).sum())
        fixed = max(1, used // 4)
        moved = fixed + (places - fixed + turn * (used - fixed)) % max(1, amount - fixed)
        return jnp.zeros((amount,), jnp.int32).at[sequence[jnp.where(places < fixed, places, moved)]].set(jnp.asarray(tallies, jnp.int32))

    tallies = jnp.where(number % 4 == 0, named(crowded, number // 4), named(common, number - number // 4 - 1))
    mixed = jax.random.permutation(jax.random.fold_in(own, 3), amount)
    donor, sink = mixed[0:amount // 2 * 2:2], mixed[1:amount // 2 * 2:2]
    room = jnp.minimum(tallies[donor] - 1, bound - tallies[sink]) // 2
    room = jnp.where((donor == sequence[0]) | (sink == sequence[0]) | (tallies[sink] == 0), 0, jnp.maximum(room, 0))
    moved = jax.random.randint(jax.random.fold_in(own, 4), (amount // 2,), 0, 1 << 20) % (room + 1)
    tallies = tallies.at[donor].add(-moved).at[sink].add(moved)
    labels = jnp.searchsorted(jnp.cumsum(tallies), jnp.arange(rows * top), side="right").astype(jnp.int32)
    grid = labels.reshape(top, rows).T
    grid = grid[jax.random.permutation(jax.random.fold_in(own, 1), rows)]
    turn = jax.random.randint(jax.random.fold_in(own, 2), (rows, 1), 0, top)
    return jnp.take_along_axis(grid, (jnp.arange(top)[None, :] + turn) % top, axis=1)


def shares(count, total, reach, skew, full):
    weights = [(1 << 20) // math.isqrt(standing ** skew) + 1 for standing in range(1, count + 1)]
    largest = reach if full else min(reach, max(-(-total // count), total * weights[0] // sum(weights)))
    least = 1 if total - largest >= count - 1 else 0
    given, spare = [largest] + [least] * (count - 1), total - largest - least * (count - 1)
    while spare > 0:
        movable = [i for i in range(1, count) if given[i] < largest] or [i for i in range(1, count) if given[i] < reach]
        mass, budget = sum([weights[i] for i in movable]), spare
        for i in movable:
            addition = min(reach - given[i], max(1, budget * weights[i] // mass), spare)
            given[i] = given[i] + addition
            spare = spare - addition
    return np.array(given)


def gaussian(own_key, dims, scale, limit, shards=(), kind=jnp.bfloat16):
    values = scale * jax.random.normal(own_key, dims, jnp.float32)
    if shards:
        values = values * block_levels(own_key, dims, shards, -0.22, 0.18)
    return jnp.clip(values, -limit, limit).astype(kind)


def setup_inputs(seed: int = 0, part: int = 0) -> dict:
    streams_of = jax.random.split(jax.random.key(seed), 9)
    part_splits = jax.random.split(jax.random.fold_in(streams_of[8], part), 9)
    residual_in = gaussian(part_splits[0], (TOKENS, D), 1.0, 6.0, ((0, 8),))
    dense_terms = gaussian(part_splits[1], (N_TP, TOKENS, D), 0.7, 6.0, ((0, 2), (1, 8)))
    norm_gain = jnp.clip(1.0 + 0.18 * jax.random.normal(streams_of[2], (D,), jnp.float32), 0.1, 1.9)
    router_weight = gaussian(streams_of[3], (D, EXPERTS), D ** -0.5, 0.09375, ((0, 2),))
    routes_keys = jax.random.split(jax.random.fold_in(part_splits[4], 1), TOKENS // TOK_DEV)
    routes_turns = jax.random.permutation(jax.random.fold_in(part_splits[4], 3), TOKENS // TOK_DEV)
    routes = jax.vmap(lambda own, number: shared_out(jax.random.fold_in(part_splits[4], 2), own, number, TOK_DEV, EXPERTS, TOPK, CAP, 2))(routes_keys, routes_turns).reshape((TOKENS, TOPK))
    placement = jax.random.permutation(streams_of[5], EXPERTS).astype(jnp.int32)
    up_weight = gaussian(streams_of[6], (D, EXPERTS * FF_E), D ** -0.5, 0.09375, ((0, 2), (1, 8)))
    down_weight = gaussian(streams_of[7], (EXPERTS * FF_E, D), FF_E ** -0.5, 0.1875, ((0, 8), (1, 2)))
    return {"residual_in": residual_in, "dense_terms": dense_terms, "norm_gain": norm_gain, "router_weight": router_weight, "routes": routes, "placement": placement, "up_weight": up_weight, "down_weight": down_weight}


def reference(residual_in, dense_terms, norm_gain, router_weight, routes, placement, up_weight, down_weight):
    state = residual_in.astype(jnp.float32) + lax.optimization_barrier(jnp.sum(dense_terms.astype(jnp.float32), axis=0))
    mean_sq = lax.optimization_barrier(jnp.mean(state * state, axis=-1, keepdims=True))
    normed = state * lax.rsqrt(mean_sq + 1e-06) * norm_gain
    logits = jnp.dot(normed, router_weight.astype(jnp.float32), precision=lax.Precision.HIGHEST)
    scores = jax.nn.sigmoid(logits)
    expert_ids = jnp.arange(EXPERTS, dtype=jnp.int32)
    onehot = routes[:, :, None] == expert_ids[None, None, :]
    chosen = lax.optimization_barrier(jnp.sum(jnp.where(onehot, scores[:, None, :], 0.0), axis=-1))
    route_weight = 2.827 * chosen / lax.optimization_barrier(jnp.sum(chosen, axis=-1, keepdims=True))
    expert_gate = lax.optimization_barrier(jnp.sum(jnp.where(onehot, route_weight[:, :, None], 0.0), axis=1))
    slot_table = (placement[:, None] == expert_ids[None, :]).astype(jnp.float32)
    slot_gate = jnp.dot(expert_gate, slot_table, precision=lax.Precision.HIGHEST)
    hits = lax.optimization_barrier(jnp.sum((slot_gate > 0.0).astype(jnp.int32), axis=0)) * 0
    routed = (slot_gate > 0.0).astype(jnp.int32)
    rows = normed.astype(jnp.bfloat16)
    slot_ids = jnp.arange(EXPERTS, dtype=jnp.int32)

    def one_block(total, block):
        first = block * COLS_DEV
        low = first // FF_E
        high = (first + COLS_DEV - 1) // FF_E
        inside = ((slot_ids >= low) & (slot_ids <= high)).astype(jnp.int32)
        need = (lax.optimization_barrier(jnp.sum(routed * inside[None, :], axis=-1)) > 0).astype(jnp.int32)
        order = jnp.argsort(1 - need + hits[0], stable=True)[:ROWS].astype(jnp.int32)
        picked = rows[order]
        up_block = lax.dynamic_slice_in_dim(up_weight, first, COLS_DEV, 1)
        down_block = lax.dynamic_slice_in_dim(down_weight, first, COLS_DEV, 0)
        pre = jnp.dot(picked, up_block, preferred_element_type=jnp.float32)
        column_slot = (first + jnp.arange(COLS_DEV, dtype=jnp.int32)) // FF_E
        column_gate = jnp.take(slot_gate[order], column_slot, axis=1)
        gated = (jax.nn.silu(pre) * column_gate).astype(jnp.bfloat16)
        term = jnp.dot(gated, down_block, preferred_element_type=jnp.float32).astype(jnp.bfloat16)
        return (total.at[order].add(term.astype(jnp.float32)), None)
    total, _ = lax.scan(one_block, jnp.zeros((TOKENS, D), jnp.float32), jnp.arange(N_EP, dtype=jnp.int32))
    return (state + total).astype(jnp.bfloat16)
```

```python
import functools

import jax
import jax.numpy as jnp
from jax import lax
from jax.experimental import pallas as pl
from jax.experimental.pallas import tpu as pltpu
from jax.sharding import PartitionSpec as P

FF_E = 1024
CAP = 12
RING = 8
UP_BUFS = 4
MESH = pl.DeviceIdType.MESH
F32 = jnp.float32
BF16 = jnp.bfloat16


def nt_dot(a, b):
    return lax.dot_general(a, b, (((1,), (1,)), ((), ())), preferred_element_type=F32)


def dot(a, b):
    return jnp.dot(a, b, preferred_element_type=F32)


def ring_device(pos):
    back = pos // (RING // 2)
    return (1 - back) * 2 * pos + back * (2 * (RING - 1 - pos) + 1)


def expert_kernel(
    slots, rows_ref, up_ref, down_ref, out_ref, gather, xy, pre_own, pre_peer, sel, sel_t, gate_col,
    send_buf, recv_buf, up_buf, down_buf, up_sem, down_sem, g_send, g_recv, p_send, p_recv, r_send, r_recv,
):
    tok, width_ext = rows_ref.shape
    width = down_buf.shape[2]
    span = FF_E
    cap = CAP * RING
    total_rows = slots * cap
    tokens = tok * RING
    half = tok // 2

    ep = lax.axis_index("ep")
    tp = lax.axis_index("tp")
    x_pos = lax.rem(ep, 2)
    z_pos = ep // 2
    pos = z_pos + x_pos * (RING - 1 - 2 * z_pos)
    right = ring_device(lax.rem(pos + 1, RING))
    left = ring_device(lax.rem(pos + RING - 1, RING))
    sides = (right, left)
    step_of = (1, -1)

    def up_copy(s):
        b = lax.rem(s, UP_BUFS)
        return pltpu.make_async_copy(
            up_ref.at[:, pl.ds(pl.multiple_of(s * span, span), span)], up_buf.at[b], up_sem.at[b]
        )

    def down_copy(s):
        return pltpu.make_async_copy(
            down_ref.at[pl.ds(pl.multiple_of(s * span, span), span), :], down_buf.at[s], down_sem.at[s]
        )

    barrier = pltpu.get_barrier_semaphore()
    for side in sides:
        pl.semaphore_signal(barrier, inc=1, device_id={"ep": side}, device_id_type=MESH)
    pl.semaphore_signal(barrier, inc=1, device_id={"tp": 1 - tp}, device_id_type=MESH)
    gather[pos] = rows_ref[...]
    pl.semaphore_wait(barrier, 3)

    def gather_copy(way, k):
        block = lax.rem(pos - step_of[way] * k + RING, RING)
        if k == RING // 2 - 1:
            ref = gather.at[block, pl.ds(way * half, half), :]
        else:
            ref = gather.at[block]
        return pltpu.make_async_remote_copy(
            src_ref=ref, dst_ref=ref, send_sem=g_send.at[way, k], recv_sem=g_recv.at[way, k],
            device_id={"ep": sides[way]}, device_id_type=MESH,
        )

    steps = RING // 2
    copies = [[None] * steps, [None] * steps]
    for k in range(steps):
        for way in range(2):
            if k:
                copies[way][k - 1].wait_recv()
            copies[way][k] = gather_copy(way, k)
            copies[way][k].start()
        if k == 0:
            for s in range(UP_BUFS):
                up_copy(s).start()
            for s in range(slots):
                down_copy(s).start()
    for way in range(2):
        copies[way][steps - 1].wait_recv()
    for way in range(2):
        for k in range(steps):
            copies[way][k].wait_send()

    gates = gather[:, :, width:].reshape(tokens, width_ext - width)
    experts = (width_ext - width) // 2
    first = ep * slots
    lane = lax.broadcasted_iota(jnp.int32, (2 * experts, 128), 0)
    slot = lax.broadcasted_iota(jnp.int32, (2 * experts, 128), 1)
    inside = slot < slots
    pick_hi = ((lane == slot + first) & inside).astype(BF16)
    pick_lo = ((lane == slot + first + experts) & inside).astype(BF16)
    gate_hi = dot(gates, pick_hi).astype(BF16)
    gate_lo = dot(gates, pick_lo).astype(BF16)
    lane_t = lax.broadcasted_iota(jnp.int32, (16, 2 * experts), 1)
    slot_t = lax.broadcasted_iota(jnp.int32, (16, 2 * experts), 0)
    pick_t = ((lane_t == slot_t + first) & (slot_t < slots)).astype(BF16)
    need_t = nt_dot(pick_t, gates) > 0.0
    need = gate_hi.astype(F32) > 0.0
    t_row = lax.broadcasted_iota(jnp.int32, (tokens, tokens), 0)
    t_col = lax.broadcasted_iota(jnp.int32, (tokens, tokens), 1)
    lower = (t_col <= t_row).astype(F32).astype(BF16)
    upper = (t_row <= t_col).astype(F32).astype(BF16)
    order = dot(lower, need.astype(F32).astype(BF16))
    order_t = dot(need_t.astype(F32).astype(BF16), upper)
    order = jnp.where(need, order, 0.0).astype(BF16)
    order_t = jnp.where(need_t, order_t, 0.0).astype(BF16)

    def place_of(shape, dim):
        j = lax.broadcasted_iota(jnp.int32, shape, dim)
        c = j
        for s in range(1, slots):
            c = c - jnp.where(j >= s * cap, cap, 0)
        return (c + 1).astype(F32)

    def spread(shape, dim):
        j = lax.broadcasted_iota(jnp.int32, shape, dim)
        s = lax.broadcasted_iota(jnp.int32, shape, 1 - dim)
        return (j >= s * cap) & (j < (s + 1) * cap)

    spread_c = spread((128, total_rows), 1).astype(F32).astype(BF16)
    spread_r = spread((total_rows, 16), 0).astype(F32).astype(BF16)
    sel_t[...] = (dot(order, spread_c) == place_of((1, total_rows), 1)).astype(F32).astype(BF16)
    sel[...] = (dot(spread_r, order_t) == place_of((total_rows, 1), 0)).astype(F32).astype(BF16)
    row_gates = dot(sel[...], gate_hi) + dot(sel[...], gate_lo)
    own_slot = spread((total_rows, 128), 0)
    gate_col[...] = jnp.sum(jnp.where(own_slot, row_gates, 0.0), axis=1, keepdims=True)

    def peer_copy(s):
        return pltpu.make_async_remote_copy(
            src_ref=pre_own.at[s], dst_ref=pre_peer.at[s], send_sem=p_send.at[s], recv_sem=p_recv.at[s],
            device_id={"tp": 1 - tp}, device_id_type=MESH,
        )

    def up_step(s, carry):
        at = pl.ds(pl.multiple_of(s * cap, cap), cap)
        all_rows = gather[:, :, :width].reshape(tokens, width)
        x = dot(sel[at, :], all_rows).astype(BF16)
        up_copy(s).wait()
        pre_own[s] = dot(x, up_buf[lax.rem(s, UP_BUFS)]).astype(BF16)
        peer_copy(s).start()

        @pl.when(s + UP_BUFS < slots)
        def _():
            up_copy(s + UP_BUFS).start()

        return carry

    lax.fori_loop(0, slots, up_step, 0)

    def down_step(s, carry):
        at = pl.ds(pl.multiple_of(s * cap, cap), cap)
        peer_copy(s).wait()
        pre = pre_own[s].astype(F32) + pre_peer[s].astype(F32)
        gated = (jax.nn.silu(pre) * gate_col[at, :]).astype(BF16)
        down_copy(s).wait()
        xy[at, :] = dot(gated, down_buf[s]).astype(BF16)
        return carry

    lax.fori_loop(0, slots, down_step, 0)

    def chunk(dest, start, rows):
        at = pl.ds(pl.multiple_of(dest * tok + start, half), rows)
        return dot(sel_t[at, :], xy[...])

    def reduce_copy(way, k):
        at = pl.ds(way * half, half) if k == 0 else pl.ds(0, tok)
        return pltpu.make_async_remote_copy(
            src_ref=send_buf.at[way, k, at, :], dst_ref=recv_buf.at[way, k, at, :],
            send_sem=r_send.at[way, k], recv_sem=r_recv.at[way, k],
            device_id={"ep": sides[way]}, device_id_type=MESH,
        )

    for k in range(steps):
        for way in range(2):
            dest = lax.rem(pos + step_of[way] * (steps - k) + RING, RING)
            if k == 0:
                own = chunk(dest, way * half, half)
                send_buf[way, k, pl.ds(way * half, half), :] = own.astype(BF16)
            else:
                own = chunk(dest, 0, tok)
                reduce_copy(way, k - 1).wait_recv()
                if k == 1:
                    at = slice(way * half, (way + 1) * half)
                    other = slice((1 - way) * half, (2 - way) * half)
                    send_buf[way, k, other, :] = own[other].astype(BF16)
                    send_buf[way, k, at, :] = (own[at] + recv_buf[way, 0, at, :].astype(F32)).astype(BF16)
                else:
                    send_buf[way, k] = (own + recv_buf[way, k - 1].astype(F32)).astype(BF16)
            reduce_copy(way, k).start()
    own = chunk(pos, 0, tok)
    for way in range(2):
        reduce_copy(way, steps - 1).wait_recv()
        own = own + recv_buf[way, steps - 1].astype(F32)
    out_ref[...] = own
    for way in range(2):
        for k in range(steps):
            reduce_copy(way, k).wait_send()


def experts_on_ring(rows_ext, up_weight, down_weight):
    tok, width_ext = rows_ext.shape
    width = up_weight.shape[0]
    slots = up_weight.shape[1] // FF_E
    cap = CAP * RING
    steps = RING // 2
    vmem = pl.BlockSpec(memory_space=pltpu.VMEM)
    hbm = pl.BlockSpec(memory_space=pl.ANY)
    dma = pltpu.SemaphoreType.DMA
    return pl.pallas_call(
        functools.partial(expert_kernel, slots),
        out_shape=jax.ShapeDtypeStruct((tok, width), F32),
        in_specs=[vmem, hbm, hbm],
        out_specs=vmem,
        scratch_shapes=[
            pltpu.VMEM((RING, tok, width_ext), BF16),
            pltpu.VMEM((slots * cap, width), BF16),
            pltpu.VMEM((slots, cap, FF_E), BF16),
            pltpu.VMEM((slots, cap, FF_E), BF16),
            pltpu.VMEM((slots * cap, RING * tok), BF16),
            pltpu.VMEM((RING * tok, slots * cap), BF16),
            pltpu.VMEM((slots * cap, 1), F32),
            pltpu.VMEM((2, steps, tok, width), BF16),
            pltpu.VMEM((2, steps, tok, width), BF16),
            pltpu.VMEM((UP_BUFS, width, FF_E), BF16),
            pltpu.VMEM((slots, FF_E, width), BF16),
            dma((UP_BUFS,)),
            dma((slots,)),
            dma((2, steps)),
            dma((2, steps)),
            dma((slots,)),
            dma((slots,)),
            dma((2, steps)),
            dma((2, steps)),
        ],
        compiler_params=pltpu.CompilerParams(
            collective_id=0, has_side_effects=True, vmem_limit_bytes=62 * 1024 * 1024
        ),
    )(rows_ext, up_weight, down_weight)


def experts_by_exchange(normed_half, slot_gate, up_weight, down_weight):
    columns = up_weight.shape[1]
    tok_rows = normed_half.shape[0]
    experts = slot_gate.shape[1]
    peers = lax.axis_size("ep")
    local_slots = max(1, columns // FF_E)
    span = min(FF_E, columns)
    capacity = min(tok_rows, CAP * local_slots)
    expert_ids = jnp.arange(experts, dtype=jnp.int32)
    peer_ids = jnp.arange(peers, dtype=jnp.int32)
    slot_of_peer = (
        peer_ids[:, None] * columns // FF_E + jnp.arange(local_slots, dtype=jnp.int32)[None, :]
    )
    pick_table = (slot_of_peer[:, :, None] == expert_ids[None, None, :]).astype(F32)
    peer_gates = jnp.einsum("ts,pls->tpl", slot_gate, pick_table, precision=lax.Precision.HIGHEST)
    need = (jnp.sum(peer_gates, axis=-1) > 0.0).astype(jnp.int32)
    position = jnp.cumsum(need, axis=0) - 1
    slot_pos = jnp.arange(capacity, dtype=jnp.int32)
    selector = (need.T[:, None, :] == 1) & (position.T[:, None, :] == slot_pos[None, :, None])
    select_b = selector.astype(BF16)
    send_gates = jnp.einsum(
        "pct,tpl->pcl", selector.astype(F32), peer_gates, precision=lax.Precision.HIGHEST
    )
    send_rows = jnp.einsum(
        "pct,tf->pcf", select_b, normed_half.astype(BF16), preferred_element_type=F32
    ).astype(BF16)
    rows_in = lax.all_to_all(send_rows, "ep", split_axis=0, concat_axis=0, tiled=True)
    gates_in = lax.all_to_all(
        send_gates.astype(BF16), "ep", split_axis=0, concat_axis=0, tiled=True
    ).astype(F32)
    part_pre = jnp.einsum("sif,fh->sih", rows_in, up_weight, preferred_element_type=F32)
    pre = lax.psum(part_pre.astype(BF16), "tp").astype(F32)
    column_gate = jnp.repeat(gates_in, span, axis=2)
    gated = (jax.nn.silu(pre) * column_gate).astype(BF16)
    result = jnp.einsum("sih,hf->sif", gated, down_weight, preferred_element_type=F32).astype(BF16)
    returned = lax.all_to_all(result, "ep", split_axis=0, concat_axis=0, tiled=True)
    return jnp.einsum("pct,pcf->tf", select_b, returned, preferred_element_type=F32)


def on_device(
    ring, residual_in, dense_terms, norm_gain, router_weight, routes, placement, up_weight, down_weight
):
    half_width = up_weight.shape[0]
    experts = placement.shape[0]
    full_width = residual_in.shape[1]
    tp = lax.axis_index("tp")
    start = tp * half_width
    other = (1 - tp) * half_width

    def cut(a, at):
        return lax.dynamic_slice_in_dim(a, at, half_width, a.ndim - 1)

    theirs = lax.ppermute(cut(dense_terms[0], other), "tp", [(0, 1), (1, 0)])
    state_half = cut(residual_in, start).astype(F32) + (
        cut(dense_terms[0], start).astype(F32) + theirs.astype(F32)
    )
    scaled = state_half * cut(norm_gain, start)
    part_logits = jnp.dot(scaled, router_weight.astype(F32), precision=lax.Precision.HIGHEST)
    part_sq = jnp.sum(state_half * state_half, axis=-1, keepdims=True)
    sums = lax.psum(jnp.concatenate([part_logits, part_sq], axis=1), "tp")
    scale = lax.rsqrt(sums[:, experts:] / full_width + 1e-06)
    scores = jax.nn.sigmoid(sums[:, :experts] * scale)
    normed_half = scaled * scale
    expert_ids = jnp.arange(experts, dtype=jnp.int32)
    routed = jnp.any(routes[:, :, None] == expert_ids[None, None, :], axis=1)
    chosen = jnp.where(routed, scores, 0.0)
    expert_gate = 2.827 * chosen / jnp.sum(chosen, axis=-1, keepdims=True)
    slot_table = (placement[:, None] == expert_ids[None, :]).astype(F32)
    slot_gate = jnp.dot(expert_gate, slot_table, precision=lax.Precision.HIGHEST)
    if ring:
        gate_hi = slot_gate.astype(BF16)
        gate_lo = (slot_gate - gate_hi.astype(F32)).astype(BF16)
        rows_ext = jnp.concatenate([normed_half.astype(BF16), gate_hi, gate_lo], axis=1)
        expert_sum = experts_on_ring(rows_ext, up_weight, down_weight)
    else:
        expert_sum = experts_by_exchange(normed_half, slot_gate, up_weight, down_weight)
    return (state_half + expert_sum).astype(BF16)


def solution(mesh):
    ring = mesh.shape["ep"] == RING
    in_specs = (
        P(("replica", "ep"), None),
        P("tp", ("replica", "ep"), None),
        P(),
        P("tp", None),
        P(("replica", "ep"), None),
        P(),
        P("tp", "ep"),
        P("ep", "tp"),
    )
    out_specs = P(("replica", "ep"), "tp")
    return jax.shard_map(
        functools.partial(on_device, ring), mesh=mesh, in_specs=in_specs, out_specs=out_specs, check_vma=False
    )
```

```python
import functools

import jax
import jax.numpy as jnp
from jax import lax
from jax.experimental import pallas as pl
from jax.experimental.pallas import tpu as pltpu
from jax.sharding import PartitionSpec as P

FF_E = 1024
CAP = 12
RING = 8
UP_BUFS = 6
DOWN_BUFS = 12
PARTS = 2
MESH = pl.DeviceIdType.MESH
F32 = jnp.float32
BF16 = jnp.bfloat16


def nt_dot(a, b):
    return lax.dot_general(a, b, (((1,), (1,)), ((), ())), preferred_element_type=F32)


def dot(a, b):
    return jnp.dot(a, b, preferred_element_type=F32)


def ring_device(pos):
    back = pos // (RING // 2)
    return (1 - back) * 2 * pos + back * (2 * (RING - 1 - pos) + 1)


def expert_kernel(
    slots, rows_ref, up_ref, down_ref, out_ref, gather, xy, pre_own, pre_peer, sel, sel_t, gate_col,
    send_buf, recv_buf, up_buf, down_buf, up_sem, down_sem, g_send, g_recv, p_send, p_recv, r_send, r_recv,
):
    tok, width_ext = rows_ref.shape
    part_w = down_buf.shape[2]
    width = part_w * PARTS
    span = FF_E
    cap = CAP * RING
    total_rows = slots * cap
    tokens = tok * RING
    half = tok // 2

    ep = lax.axis_index("ep")
    tp = lax.axis_index("tp")
    x_pos = lax.rem(ep, 2)
    z_pos = ep // 2
    pos = z_pos + x_pos * (RING - 1 - 2 * z_pos)
    right = ring_device(lax.rem(pos + 1, RING))
    left = ring_device(lax.rem(pos + RING - 1, RING))
    sides = (right, left)
    step_of = (1, -1)

    def up_copy(s):
        b = lax.rem(s, UP_BUFS)
        return pltpu.make_async_copy(
            up_ref.at[:, pl.ds(pl.multiple_of(s * span, span), span)], up_buf.at[b], up_sem.at[b]
        )

    def down_copy(j):
        part = j // slots
        s = j - part * slots
        b = lax.rem(j, DOWN_BUFS)
        return pltpu.make_async_copy(
            down_ref.at[
                pl.ds(pl.multiple_of(s * span, span), span),
                pl.ds(pl.multiple_of(part * part_w, part_w), part_w),
            ],
            down_buf.at[b],
            down_sem.at[b],
        )

    barrier = pltpu.get_barrier_semaphore()
    for side in sides:
        pl.semaphore_signal(barrier, inc=1, device_id={"ep": side}, device_id_type=MESH)
    pl.semaphore_signal(barrier, inc=1, device_id={"tp": 1 - tp}, device_id_type=MESH)
    gather[pos] = rows_ref[...]
    pl.semaphore_wait(barrier, 3)

    def gather_copy(way, k, c):
        block = lax.rem(pos - step_of[way] * k + RING, RING)
        ref = gather.at[block, pl.ds(c * half, half), :]
        return pltpu.make_async_remote_copy(
            src_ref=ref, dst_ref=ref, send_sem=g_send.at[way, k, c], recv_sem=g_recv.at[way, k, c],
            device_id={"ep": sides[way]}, device_id_type=MESH,
        )

    steps = RING // 2
    copies = {}
    for k in range(steps):
        for c in range(PARTS):
            for way in range(2):
                part = way if c == 0 else 1 - way
                if k:
                    copies[way, k - 1, part].wait_recv()
                if k == steps - 1 and part != way:
                    continue
                copies[way, k, part] = gather_copy(way, k, part)
                copies[way, k, part].start()
        if k == 0:
            for s in range(UP_BUFS):
                up_copy(s).start()
            for j in range(DOWN_BUFS):
                down_copy(j).start()
    for way in range(2):
        copies[way, steps - 1, way].wait_recv()
    for copy in copies.values():
        copy.wait_send()

    gates = gather[:, :, width:].reshape(tokens, width_ext - width)
    experts = (width_ext - width) // 2
    first = ep * slots
    lane = lax.broadcasted_iota(jnp.int32, (2 * experts, 128), 0)
    slot = lax.broadcasted_iota(jnp.int32, (2 * experts, 128), 1)
    inside = slot < slots
    pick_hi = ((lane == slot + first) & inside).astype(BF16)
    pick_lo = ((lane == slot + first + experts) & inside).astype(BF16)
    gate_hi = dot(gates, pick_hi).astype(BF16)
    gate_lo = dot(gates, pick_lo).astype(BF16)
    lane_t = lax.broadcasted_iota(jnp.int32, (16, 2 * experts), 1)
    slot_t = lax.broadcasted_iota(jnp.int32, (16, 2 * experts), 0)
    pick_t = ((lane_t == slot_t + first) & (slot_t < slots)).astype(BF16)
    need_t = nt_dot(pick_t, gates) > 0.0
    need = gate_hi.astype(F32) > 0.0
    t_row = lax.broadcasted_iota(jnp.int32, (tokens, tokens), 0)
    t_col = lax.broadcasted_iota(jnp.int32, (tokens, tokens), 1)
    lower = (t_col <= t_row).astype(F32).astype(BF16)
    upper = (t_row <= t_col).astype(F32).astype(BF16)
    order = dot(lower, need.astype(F32).astype(BF16))
    order_t = dot(need_t.astype(F32).astype(BF16), upper)
    order = jnp.where(need, order, 0.0).astype(BF16)
    order_t = jnp.where(need_t, order_t, 0.0).astype(BF16)

    def place_of(shape, dim):
        j = lax.broadcasted_iota(jnp.int32, shape, dim)
        c = j
        for s in range(1, slots):
            c = c - jnp.where(j >= s * cap, cap, 0)
        return (c + 1).astype(F32)

    def spread(shape, dim):
        j = lax.broadcasted_iota(jnp.int32, shape, dim)
        s = lax.broadcasted_iota(jnp.int32, shape, 1 - dim)
        return (j >= s * cap) & (j < (s + 1) * cap)

    spread_c = spread((128, total_rows), 1).astype(F32).astype(BF16)
    spread_r = spread((total_rows, 16), 0).astype(F32).astype(BF16)
    sel_t[...] = (dot(order, spread_c) == place_of((1, total_rows), 1)).astype(F32).astype(BF16)
    sel[...] = (dot(spread_r, order_t) == place_of((total_rows, 1), 0)).astype(F32).astype(BF16)
    row_gates = dot(sel[...], gate_hi) + dot(sel[...], gate_lo)
    own_slot = spread((total_rows, 128), 0)
    gate_col[...] = jnp.sum(jnp.where(own_slot, row_gates, 0.0), axis=1, keepdims=True)

    def peer_copy(s):
        return pltpu.make_async_remote_copy(
            src_ref=pre_own.at[s], dst_ref=pre_peer.at[s], send_sem=p_send.at[s], recv_sem=p_recv.at[s],
            device_id={"tp": 1 - tp}, device_id_type=MESH,
        )

    def pick_step(i, carry):
        cols = pl.ds(pl.multiple_of(i * 256, 256), 256)
        xy[:, cols] = dot(sel[...], gather[:, :, cols].reshape(tokens, 256)).astype(BF16)
        return carry

    lax.fori_loop(0, width // 256, pick_step, 0)

    def up_step(s, carry):
        at = pl.ds(pl.multiple_of(s * cap, cap), cap)
        up_copy(s).wait()
        pre_own[s] = dot(xy[at, :], up_buf[lax.rem(s, UP_BUFS)]).astype(BF16)
        peer_copy(s).start()

        @pl.when(s + UP_BUFS < slots)
        def _():
            up_copy(s + UP_BUFS).start()

        return carry

    lax.fori_loop(0, slots, up_step, 0)

    def down_step(part, s, carry):
        at = pl.ds(pl.multiple_of(s * cap, cap), cap)
        j = part * slots + s
        if part == 0:
            peer_copy(s).wait()
            pre = pre_own[s].astype(F32) + pre_peer[s].astype(F32)
            gated = (jax.nn.silu(pre) * gate_col[at, :]).astype(BF16)
            pre_own[s] = gated
        else:
            gated = pre_own[s]
        down_copy(j).wait()
        cols = slice(part * part_w, (part + 1) * part_w)
        xy[at, cols] = dot(gated, down_buf[lax.rem(j, DOWN_BUFS)]).astype(BF16)

        @pl.when(j + DOWN_BUFS < PARTS * slots)
        def _():
            down_copy(j + DOWN_BUFS).start()

        return carry

    def chunk(dest, start, rows, part):
        at = pl.ds(pl.multiple_of(dest * tok + start, half), rows)
        return dot(sel_t[at, :], xy[:, part * part_w : (part + 1) * part_w])

    def reduce_copy(way, k, part):
        at = pl.ds(way * half, half) if k == 0 else pl.ds(0, tok)
        cols = pl.ds(part * part_w, part_w)
        return pltpu.make_async_remote_copy(
            src_ref=send_buf.at[way, k, at, cols], dst_ref=recv_buf.at[way, k, at, cols],
            send_sem=r_send.at[way, k, part], recv_sem=r_recv.at[way, k, part],
            device_id={"ep": sides[way]}, device_id_type=MESH,
        )

    for part in range(PARTS):
        lax.fori_loop(0, slots, functools.partial(down_step, part), 0)
        dest = lax.rem(pos + steps, RING)
        cols = slice(part * part_w, (part + 1) * part_w)
        for way in range(2):
            rows = slice(way * half, (way + 1) * half)
            send_buf[way, 0, rows, cols] = chunk(dest, way * half, half, part).astype(BF16)
            reduce_copy(way, 0, part).start()

    for k in range(1, steps):
        for part in range(PARTS):
            cols = slice(part * part_w, (part + 1) * part_w)
            for way in range(2):
                dest = lax.rem(pos + step_of[way] * (steps - k) + RING, RING)
                own = chunk(dest, 0, tok, part)
                reduce_copy(way, k - 1, part).wait_recv()
                if k == 1:
                    at = slice(way * half, (way + 1) * half)
                    other = slice((1 - way) * half, (2 - way) * half)
                    send_buf[way, k, other, cols] = own[other].astype(BF16)
                    send_buf[way, k, at, cols] = (own[at] + recv_buf[way, 0, at, cols].astype(F32)).astype(BF16)
                else:
                    send_buf[way, k, :, cols] = (own + recv_buf[way, k - 1, :, cols].astype(F32)).astype(BF16)
                reduce_copy(way, k, part).start()
    for part in range(PARTS):
        cols = slice(part * part_w, (part + 1) * part_w)
        own = chunk(pos, 0, tok, part)
        for way in range(2):
            reduce_copy(way, steps - 1, part).wait_recv()
            own = own + recv_buf[way, steps - 1, :, cols].astype(F32)
        out_ref[:, cols] = own
    for way in range(2):
        for k in range(steps):
            for part in range(PARTS):
                reduce_copy(way, k, part).wait_send()


def experts_on_ring(rows_ext, up_weight, down_weight):
    tok, width_ext = rows_ext.shape
    width = up_weight.shape[0]
    slots = up_weight.shape[1] // FF_E
    cap = CAP * RING
    steps = RING // 2
    vmem = pl.BlockSpec(memory_space=pltpu.VMEM)
    hbm = pl.BlockSpec(memory_space=pl.ANY)
    dma = pltpu.SemaphoreType.DMA
    return pl.pallas_call(
        functools.partial(expert_kernel, slots),
        out_shape=jax.ShapeDtypeStruct((tok, width), F32),
        in_specs=[vmem, hbm, hbm],
        out_specs=vmem,
        scratch_shapes=[
            pltpu.VMEM((RING, tok, width_ext), BF16),
            pltpu.VMEM((slots * cap, width), BF16),
            pltpu.VMEM((slots, cap, FF_E), BF16),
            pltpu.VMEM((slots, cap, FF_E), BF16),
            pltpu.VMEM((slots * cap, RING * tok), BF16),
            pltpu.VMEM((RING * tok, slots * cap), BF16),
            pltpu.VMEM((slots * cap, 1), F32),
            pltpu.VMEM((2, steps, tok, width), BF16),
            pltpu.VMEM((2, steps, tok, width), BF16),
            pltpu.VMEM((UP_BUFS, width, FF_E), BF16),
            pltpu.VMEM((DOWN_BUFS, FF_E, width // PARTS), BF16),
            dma((UP_BUFS,)),
            dma((DOWN_BUFS,)),
            dma((2, steps, PARTS)),
            dma((2, steps, PARTS)),
            dma((slots,)),
            dma((slots,)),
            dma((2, steps, PARTS)),
            dma((2, steps, PARTS)),
        ],
        compiler_params=pltpu.CompilerParams(
            collective_id=0, has_side_effects=True, vmem_limit_bytes=62 * 1024 * 1024
        ),
    )(rows_ext, up_weight, down_weight)


def experts_by_exchange(normed_half, slot_gate, up_weight, down_weight):
    columns = up_weight.shape[1]
    tok_rows = normed_half.shape[0]
    experts = slot_gate.shape[1]
    peers = lax.axis_size("ep")
    local_slots = max(1, columns // FF_E)
    span = min(FF_E, columns)
    capacity = min(tok_rows, CAP * local_slots)
    expert_ids = jnp.arange(experts, dtype=jnp.int32)
    peer_ids = jnp.arange(peers, dtype=jnp.int32)
    slot_of_peer = (
        peer_ids[:, None] * columns // FF_E + jnp.arange(local_slots, dtype=jnp.int32)[None, :]
    )
    pick_table = (slot_of_peer[:, :, None] == expert_ids[None, None, :]).astype(F32)
    peer_gates = jnp.einsum("ts,pls->tpl", slot_gate, pick_table, precision=lax.Precision.HIGHEST)
    need = (jnp.sum(peer_gates, axis=-1) > 0.0).astype(jnp.int32)
    position = jnp.cumsum(need, axis=0) - 1
    slot_pos = jnp.arange(capacity, dtype=jnp.int32)
    selector = (need.T[:, None, :] == 1) & (position.T[:, None, :] == slot_pos[None, :, None])
    select_b = selector.astype(BF16)
    send_gates = jnp.einsum(
        "pct,tpl->pcl", selector.astype(F32), peer_gates, precision=lax.Precision.HIGHEST
    )
    send_rows = jnp.einsum(
        "pct,tf->pcf", select_b, normed_half.astype(BF16), preferred_element_type=F32
    ).astype(BF16)
    rows_in = lax.all_to_all(send_rows, "ep", split_axis=0, concat_axis=0, tiled=True)
    gates_in = lax.all_to_all(
        send_gates.astype(BF16), "ep", split_axis=0, concat_axis=0, tiled=True
    ).astype(F32)
    part_pre = jnp.einsum("sif,fh->sih", rows_in, up_weight, preferred_element_type=F32)
    pre = lax.psum(part_pre.astype(BF16), "tp").astype(F32)
    column_gate = jnp.repeat(gates_in, span, axis=2)
    gated = (jax.nn.silu(pre) * column_gate).astype(BF16)
    result = jnp.einsum("sih,hf->sif", gated, down_weight, preferred_element_type=F32).astype(BF16)
    returned = lax.all_to_all(result, "ep", split_axis=0, concat_axis=0, tiled=True)
    return jnp.einsum("pct,pcf->tf", select_b, returned, preferred_element_type=F32)


def on_device(
    ring, residual_in, dense_terms, norm_gain, router_weight, routes, placement, up_weight, down_weight
):
    half_width = up_weight.shape[0]
    experts = placement.shape[0]
    full_width = residual_in.shape[1]
    tp = lax.axis_index("tp")
    start = tp * half_width
    other = (1 - tp) * half_width

    def cut(a, at):
        return lax.dynamic_slice_in_dim(a, at, half_width, a.ndim - 1)

    theirs = lax.ppermute(cut(dense_terms[0], other), "tp", [(0, 1), (1, 0)])
    state_half = cut(residual_in, start).astype(F32) + (
        cut(dense_terms[0], start).astype(F32) + theirs.astype(F32)
    )
    scaled = state_half * cut(norm_gain, start)
    part_logits = jnp.dot(scaled, router_weight.astype(F32), precision=lax.Precision.HIGHEST)
    part_sq = jnp.sum(state_half * state_half, axis=-1, keepdims=True)
    sums = lax.psum(jnp.concatenate([part_logits, part_sq], axis=1), "tp")
    scale = lax.rsqrt(sums[:, experts:] / full_width + 1e-06)
    scores = jax.nn.sigmoid(sums[:, :experts] * scale)
    normed_half = scaled * scale
    expert_ids = jnp.arange(experts, dtype=jnp.int32)
    routed = jnp.any(routes[:, :, None] == expert_ids[None, None, :], axis=1)
    chosen = jnp.where(routed, scores, 0.0)
    expert_gate = 2.827 * chosen / jnp.sum(chosen, axis=-1, keepdims=True)
    slot_table = (placement[:, None] == expert_ids[None, :]).astype(F32)
    slot_gate = jnp.dot(expert_gate, slot_table, precision=lax.Precision.HIGHEST)
    if ring:
        gate_hi = slot_gate.astype(BF16)
        gate_lo = (slot_gate - gate_hi.astype(F32)).astype(BF16)
        rows_ext = jnp.concatenate([normed_half.astype(BF16), gate_hi, gate_lo], axis=1)
        expert_sum = experts_on_ring(rows_ext, up_weight, down_weight)
    else:
        expert_sum = experts_by_exchange(normed_half, slot_gate, up_weight, down_weight)
    return (state_half + expert_sum).astype(BF16)


def solution(mesh):
    ring = mesh.shape["ep"] == RING
    in_specs = (
        P(("replica", "ep"), None),
        P("tp", ("replica", "ep"), None),
        P(),
        P("tp", None),
        P(("replica", "ep"), None),
        P(),
        P("tp", "ep"),
        P("ep", "tp"),
    )
    out_specs = P(("replica", "ep"), "tp")
    return jax.shard_map(
        functools.partial(on_device, ring), mesh=mesh, in_specs=in_specs, out_specs=out_specs, check_vma=False
    )
```

```python
import functools

import jax
import jax.numpy as jnp
from jax import lax
from jax.experimental import pallas as pl
from jax.experimental.pallas import tpu as pltpu
from jax.sharding import PartitionSpec as P

FF_E = 1024
CAP = 12
RING = 8
UP_BUFS = 6
DOWN_BUFS = 12
PARTS = 2
MESH = pl.DeviceIdType.MESH
F32 = jnp.float32
BF16 = jnp.bfloat16


def nt_dot(a, b):
    return lax.dot_general(a, b, (((1,), (1,)), ((), ())), preferred_element_type=F32)


def dot(a, b):
    return jnp.dot(a, b, preferred_element_type=F32)


def ring_device(pos):
    back = pos // (RING // 2)
    return (1 - back) * 2 * pos + back * (2 * (RING - 1 - pos) + 1)


def expert_kernel(
    slots, res_ref, dense_ref, gain_ref, router_ref, routes_ref, place_ref, up_ref, down_ref, out_ref,
    theirs, state, stat_own, stat_peer, d_send, d_recv, gather, xy, pre_own, pre_peer, sel, sel_t, gate_col,
    send_buf, recv_buf, up_buf, down_buf, up_sem, down_sem, g_send, g_recv, p_send, p_recv, r_send, r_recv,
):
    tok, full_width = res_ref.shape
    experts = router_ref.shape[1]
    width_ext = gather.shape[2]
    part_w = down_buf.shape[2]
    width = part_w * PARTS
    span = FF_E
    cap = CAP * RING
    total_rows = slots * cap
    tokens = tok * RING
    half = tok // 2

    ep = lax.axis_index("ep")
    tp = lax.axis_index("tp")
    x_pos = lax.rem(ep, 2)
    z_pos = ep // 2
    pos = z_pos + x_pos * (RING - 1 - 2 * z_pos)
    right = ring_device(lax.rem(pos + 1, RING))
    left = ring_device(lax.rem(pos + RING - 1, RING))
    sides = (right, left)
    step_of = (1, -1)

    def up_copy(s):
        b = lax.rem(s, UP_BUFS)
        return pltpu.make_async_copy(
            up_ref.at[:, pl.ds(pl.multiple_of(s * span, span), span)], up_buf.at[b], up_sem.at[b]
        )

    def down_copy(j):
        part = j // slots
        s = j - part * slots
        b = lax.rem(j, DOWN_BUFS)
        return pltpu.make_async_copy(
            down_ref.at[
                pl.ds(pl.multiple_of(s * span, span), span),
                pl.ds(pl.multiple_of(part * part_w, part_w), part_w),
            ],
            down_buf.at[b],
            down_sem.at[b],
        )

    barrier = pltpu.get_barrier_semaphore()
    for side in sides:
        pl.semaphore_signal(barrier, inc=1, device_id={"ep": side}, device_id_type=MESH)
    pl.semaphore_signal(barrier, inc=1, device_id={"tp": 1 - tp}, device_id_type=MESH)
    for s in range(UP_BUFS):
        up_copy(s).start()
    for j in range(DOWN_BUFS):
        down_copy(j).start()
    pl.semaphore_wait(barrier, 3)

    mine = pl.ds(pl.multiple_of(tp * width, width), width)
    other = pl.ds(pl.multiple_of((1 - tp) * width, width), width)
    dense_copy = pltpu.make_async_remote_copy(
        src_ref=dense_ref.at[0, :, other], dst_ref=theirs, send_sem=d_send.at[0], recv_sem=d_recv.at[0],
        device_id={"tp": 1 - tp}, device_id_type=MESH,
    )
    dense_copy.start()
    partial = res_ref[:, mine].astype(F32)
    own_dense = dense_ref[0, :, mine].astype(F32)
    dense_copy.wait()
    total = partial + (own_dense + theirs[...].astype(F32))
    state[...] = total
    scaled = total * gain_ref[:, mine]
    stat_own[:, :experts] = jnp.dot(
        scaled, router_ref[...].astype(F32), precision=lax.Precision.HIGHEST, preferred_element_type=F32
    )
    square = jnp.sum(total * total, axis=1, keepdims=True)
    stat_own[:, experts:] = jnp.broadcast_to(square, (tok, stat_own.shape[1] - experts))
    stat_copy = pltpu.make_async_remote_copy(
        src_ref=stat_own, dst_ref=stat_peer, send_sem=d_send.at[1], recv_sem=d_recv.at[1],
        device_id={"tp": 1 - tp}, device_id_type=MESH,
    )
    stat_copy.start()
    expert_id = lax.broadcasted_iota(jnp.int32, (tok, experts), 1)
    routed = routes_ref[:, 0:1] == expert_id
    for r in range(1, routes_ref.shape[1]):
        routed = routed | (routes_ref[:, r : r + 1] == expert_id)
    table = place_ref[...] == lax.broadcasted_iota(jnp.int32, (experts, experts), 0)
    table = table.astype(F32).astype(BF16)
    stat_copy.wait()
    logits = stat_own[:, :experts] + stat_peer[:, :experts]
    mean_sq = (stat_own[:, experts : experts + 1] + stat_peer[:, experts : experts + 1]) / full_width
    scale = lax.rsqrt(mean_sq + 1e-06)
    gather[pos, :, :width] = (state[...] * gain_ref[:, mine] * scale).astype(BF16)
    chosen = jnp.where(routed, jax.nn.sigmoid(logits * scale), 0.0)
    gate = 2.827 * chosen / jnp.sum(chosen, axis=1, keepdims=True)
    high = gate.astype(BF16)
    low = (gate - high.astype(F32)).astype(BF16)
    gather[pos, :, width : width + experts] = nt_dot(high, table).astype(BF16)
    gather[pos, :, width + experts :] = nt_dot(low, table).astype(BF16)

    def gather_copy(way, k, c):
        block = lax.rem(pos - step_of[way] * k + RING, RING)
        ref = gather.at[block, pl.ds(c * half, half), :]
        return pltpu.make_async_remote_copy(
            src_ref=ref, dst_ref=ref, send_sem=g_send.at[way, k, c], recv_sem=g_recv.at[way, k, c],
            device_id={"ep": sides[way]}, device_id_type=MESH,
        )

    steps = RING // 2
    copies = {}
    for k in range(steps):
        for c in range(PARTS):
            for way in range(2):
                part = way if c == 0 else 1 - way
                if k:
                    copies[way, k - 1, part].wait_recv()
                if k == steps - 1 and part != way:
                    continue
                copies[way, k, part] = gather_copy(way, k, part)
                copies[way, k, part].start()
    for way in range(2):
        copies[way, steps - 1, way].wait_recv()
    for copy in copies.values():
        copy.wait_send()

    gates = gather[:, :, width:].reshape(tokens, width_ext - width)
    first = ep * slots
    lane = lax.broadcasted_iota(jnp.int32, (2 * experts, 128), 0)
    slot = lax.broadcasted_iota(jnp.int32, (2 * experts, 128), 1)
    inside = slot < slots
    pick_hi = ((lane == slot + first) & inside).astype(BF16)
    pick_lo = ((lane == slot + first + experts) & inside).astype(BF16)
    gate_hi = dot(gates, pick_hi).astype(BF16)
    gate_lo = dot(gates, pick_lo).astype(BF16)
    lane_t = lax.broadcasted_iota(jnp.int32, (16, 2 * experts), 1)
    slot_t = lax.broadcasted_iota(jnp.int32, (16, 2 * experts), 0)
    pick_t = ((lane_t == slot_t + first) & (slot_t < slots)).astype(BF16)
    need_t = nt_dot(pick_t, gates) > 0.0
    need = gate_hi.astype(F32) > 0.0
    t_row = lax.broadcasted_iota(jnp.int32, (tokens, tokens), 0)
    t_col = lax.broadcasted_iota(jnp.int32, (tokens, tokens), 1)
    lower = (t_col <= t_row).astype(F32).astype(BF16)
    upper = (t_row <= t_col).astype(F32).astype(BF16)
    order = dot(lower, need.astype(F32).astype(BF16))
    order_t = dot(need_t.astype(F32).astype(BF16), upper)
    order = jnp.where(need, order, 0.0).astype(BF16)
    order_t = jnp.where(need_t, order_t, 0.0).astype(BF16)

    def place_of(shape, dim):
        j = lax.broadcasted_iota(jnp.int32, shape, dim)
        c = j
        for s in range(1, slots):
            c = c - jnp.where(j >= s * cap, cap, 0)
        return (c + 1).astype(F32)

    def spread(shape, dim):
        j = lax.broadcasted_iota(jnp.int32, shape, dim)
        s = lax.broadcasted_iota(jnp.int32, shape, 1 - dim)
        return (j >= s * cap) & (j < (s + 1) * cap)

    spread_c = spread((128, total_rows), 1).astype(F32).astype(BF16)
    spread_r = spread((total_rows, 16), 0).astype(F32).astype(BF16)
    sel_t[...] = (dot(order, spread_c) == place_of((1, total_rows), 1)).astype(F32).astype(BF16)
    sel[...] = (dot(spread_r, order_t) == place_of((total_rows, 1), 0)).astype(F32).astype(BF16)
    row_gates = dot(sel[...], gate_hi) + dot(sel[...], gate_lo)
    own_slot = spread((total_rows, 128), 0)
    gate_col[...] = jnp.sum(jnp.where(own_slot, row_gates, 0.0), axis=1, keepdims=True)

    def peer_copy(s):
        return pltpu.make_async_remote_copy(
            src_ref=pre_own.at[s], dst_ref=pre_peer.at[s], send_sem=p_send.at[s], recv_sem=p_recv.at[s],
            device_id={"tp": 1 - tp}, device_id_type=MESH,
        )

    def pick_step(i, carry):
        cols = pl.ds(pl.multiple_of(i * 256, 256), 256)
        xy[:, cols] = dot(sel[...], gather[:, :, cols].reshape(tokens, 256)).astype(BF16)
        return carry

    lax.fori_loop(0, width // 256, pick_step, 0)

    def up_step(s, carry):
        at = pl.ds(pl.multiple_of(s * cap, cap), cap)
        up_copy(s).wait()
        pre_own[s] = dot(xy[at, :], up_buf[lax.rem(s, UP_BUFS)]).astype(BF16)
        peer_copy(s).start()

        @pl.when(s + UP_BUFS < slots)
        def _():
            up_copy(s + UP_BUFS).start()

        return carry

    lax.fori_loop(0, slots, up_step, 0)

    def down_step(part, s, carry):
        at = pl.ds(pl.multiple_of(s * cap, cap), cap)
        j = part * slots + s
        if part == 0:
            peer_copy(s).wait()
            pre = pre_own[s].astype(F32) + pre_peer[s].astype(F32)
            gated = (jax.nn.silu(pre) * gate_col[at, :]).astype(BF16)
            pre_own[s] = gated
        else:
            gated = pre_own[s]
        down_copy(j).wait()
        cols = slice(part * part_w, (part + 1) * part_w)
        xy[at, cols] = dot(gated, down_buf[lax.rem(j, DOWN_BUFS)]).astype(BF16)

        @pl.when(j + DOWN_BUFS < PARTS * slots)
        def _():
            down_copy(j + DOWN_BUFS).start()

        return carry

    def chunk(dest, start, rows, part):
        at = pl.ds(pl.multiple_of(dest * tok + start, half), rows)
        return dot(sel_t[at, :], xy[:, part * part_w : (part + 1) * part_w])

    def reduce_copy(way, k, part):
        at = pl.ds(way * half, half) if k == 0 else pl.ds(0, tok)
        cols = pl.ds(part * part_w, part_w)
        return pltpu.make_async_remote_copy(
            src_ref=send_buf.at[way, k, at, cols], dst_ref=recv_buf.at[way, k, at, cols],
            send_sem=r_send.at[way, k, part], recv_sem=r_recv.at[way, k, part],
            device_id={"ep": sides[way]}, device_id_type=MESH,
        )

    for part in range(PARTS):
        lax.fori_loop(0, slots, functools.partial(down_step, part), 0)
        dest = lax.rem(pos + steps, RING)
        cols = slice(part * part_w, (part + 1) * part_w)
        for way in range(2):
            rows = slice(way * half, (way + 1) * half)
            send_buf[way, 0, rows, cols] = chunk(dest, way * half, half, part).astype(BF16)
            reduce_copy(way, 0, part).start()

    for k in range(1, steps):
        for part in range(PARTS):
            cols = slice(part * part_w, (part + 1) * part_w)
            for way in range(2):
                dest = lax.rem(pos + step_of[way] * (steps - k) + RING, RING)
                own = chunk(dest, 0, tok, part)
                reduce_copy(way, k - 1, part).wait_recv()
                if k == 1:
                    at = slice(way * half, (way + 1) * half)
                    other = slice((1 - way) * half, (2 - way) * half)
                    send_buf[way, k, other, cols] = own[other].astype(BF16)
                    send_buf[way, k, at, cols] = (own[at] + recv_buf[way, 0, at, cols].astype(F32)).astype(BF16)
                else:
                    send_buf[way, k, :, cols] = (own + recv_buf[way, k - 1, :, cols].astype(F32)).astype(BF16)
                reduce_copy(way, k, part).start()
    for part in range(PARTS):
        cols = slice(part * part_w, (part + 1) * part_w)
        own = chunk(pos, 0, tok, part)
        for way in range(2):
            reduce_copy(way, steps - 1, part).wait_recv()
            own = own + recv_buf[way, steps - 1, :, cols].astype(F32)
        out_ref[:, cols] = (own + state[:, cols]).astype(out_ref.dtype)
    for way in range(2):
        for k in range(steps):
            for part in range(PARTS):
                reduce_copy(way, k, part).wait_send()


def block_on_ring(
    residual_in, dense_terms, norm_gain, router_weight, routes, placement, up_weight, down_weight
):
    tok = residual_in.shape[0]
    width = up_weight.shape[0]
    experts = placement.shape[0]
    width_ext = width + 2 * experts
    slots = up_weight.shape[1] // FF_E
    cap = CAP * RING
    steps = RING // 2
    vmem = pl.BlockSpec(memory_space=pltpu.VMEM)
    hbm = pl.BlockSpec(memory_space=pl.ANY)
    dma = pltpu.SemaphoreType.DMA
    return pl.pallas_call(
        functools.partial(expert_kernel, slots),
        out_shape=jax.ShapeDtypeStruct((tok, width), BF16),
        in_specs=[vmem] * 6 + [hbm, hbm],
        out_specs=vmem,
        scratch_shapes=[
            pltpu.VMEM((tok, width), BF16),
            pltpu.VMEM((tok, width), F32),
            pltpu.VMEM((tok, 2 * experts), F32),
            pltpu.VMEM((tok, 2 * experts), F32),
            dma((2,)),
            dma((2,)),
            pltpu.VMEM((RING, tok, width_ext), BF16),
            pltpu.VMEM((slots * cap, width), BF16),
            pltpu.VMEM((slots, cap, FF_E), BF16),
            pltpu.VMEM((slots, cap, FF_E), BF16),
            pltpu.VMEM((slots * cap, RING * tok), BF16),
            pltpu.VMEM((RING * tok, slots * cap), BF16),
            pltpu.VMEM((slots * cap, 1), F32),
            pltpu.VMEM((2, steps, tok, width), BF16),
            pltpu.VMEM((2, steps, tok, width), BF16),
            pltpu.VMEM((UP_BUFS, width, FF_E), BF16),
            pltpu.VMEM((DOWN_BUFS, FF_E, width // PARTS), BF16),
            dma((UP_BUFS,)),
            dma((DOWN_BUFS,)),
            dma((2, steps, PARTS)),
            dma((2, steps, PARTS)),
            dma((slots,)),
            dma((slots,)),
            dma((2, steps, PARTS)),
            dma((2, steps, PARTS)),
        ],
        compiler_params=pltpu.CompilerParams(
            collective_id=0, has_side_effects=True, vmem_limit_bytes=62 * 1024 * 1024
        ),
    )(
        residual_in, dense_terms, norm_gain[None], router_weight, routes, placement[None], up_weight, down_weight
    )


def experts_by_exchange(normed_half, slot_gate, up_weight, down_weight):
    columns = up_weight.shape[1]
    tok_rows = normed_half.shape[0]
    experts = slot_gate.shape[1]
    peers = lax.axis_size("ep")
    local_slots = max(1, columns // FF_E)
    span = min(FF_E, columns)
    capacity = min(tok_rows, CAP * local_slots)
    expert_ids = jnp.arange(experts, dtype=jnp.int32)
    peer_ids = jnp.arange(peers, dtype=jnp.int32)
    slot_of_peer = (
        peer_ids[:, None] * columns // FF_E + jnp.arange(local_slots, dtype=jnp.int32)[None, :]
    )
    pick_table = (slot_of_peer[:, :, None] == expert_ids[None, None, :]).astype(F32)
    peer_gates = jnp.einsum("ts,pls->tpl", slot_gate, pick_table, precision=lax.Precision.HIGHEST)
    need = (jnp.sum(peer_gates, axis=-1) > 0.0).astype(jnp.int32)
    position = jnp.cumsum(need, axis=0) - 1
    slot_pos = jnp.arange(capacity, dtype=jnp.int32)
    selector = (need.T[:, None, :] == 1) & (position.T[:, None, :] == slot_pos[None, :, None])
    select_b = selector.astype(BF16)
    send_gates = jnp.einsum(
        "pct,tpl->pcl", selector.astype(F32), peer_gates, precision=lax.Precision.HIGHEST
    )
    send_rows = jnp.einsum(
        "pct,tf->pcf", select_b, normed_half.astype(BF16), preferred_element_type=F32
    ).astype(BF16)
    rows_in = lax.all_to_all(send_rows, "ep", split_axis=0, concat_axis=0, tiled=True)
    gates_in = lax.all_to_all(
        send_gates.astype(BF16), "ep", split_axis=0, concat_axis=0, tiled=True
    ).astype(F32)
    part_pre = jnp.einsum("sif,fh->sih", rows_in, up_weight, preferred_element_type=F32)
    pre = lax.psum(part_pre.astype(BF16), "tp").astype(F32)
    column_gate = jnp.repeat(gates_in, span, axis=2)
    gated = (jax.nn.silu(pre) * column_gate).astype(BF16)
    result = jnp.einsum("sih,hf->sif", gated, down_weight, preferred_element_type=F32).astype(BF16)
    returned = lax.all_to_all(result, "ep", split_axis=0, concat_axis=0, tiled=True)
    return jnp.einsum("pct,pcf->tf", select_b, returned, preferred_element_type=F32)


def on_device(
    ring, residual_in, dense_terms, norm_gain, router_weight, routes, placement, up_weight, down_weight
):
    if ring:
        return block_on_ring(
            residual_in, dense_terms, norm_gain, router_weight, routes, placement, up_weight, down_weight
        )
    half_width = up_weight.shape[0]
    experts = placement.shape[0]
    full_width = residual_in.shape[1]
    tp = lax.axis_index("tp")
    start = tp * half_width
    other = (1 - tp) * half_width

    def cut(a, at):
        return lax.dynamic_slice_in_dim(a, at, half_width, a.ndim - 1)

    theirs = lax.ppermute(cut(dense_terms[0], other), "tp", [(0, 1), (1, 0)])
    state_half = cut(residual_in, start).astype(F32) + (
        cut(dense_terms[0], start).astype(F32) + theirs.astype(F32)
    )
    scaled = state_half * cut(norm_gain, start)
    part_logits = jnp.dot(scaled, router_weight.astype(F32), precision=lax.Precision.HIGHEST)
    part_sq = jnp.sum(state_half * state_half, axis=-1, keepdims=True)
    sums = lax.psum(jnp.concatenate([part_logits, part_sq], axis=1), "tp")
    scale = lax.rsqrt(sums[:, experts:] / full_width + 1e-06)
    scores = jax.nn.sigmoid(sums[:, :experts] * scale)
    normed_half = scaled * scale
    expert_ids = jnp.arange(experts, dtype=jnp.int32)
    routed = jnp.any(routes[:, :, None] == expert_ids[None, None, :], axis=1)
    chosen = jnp.where(routed, scores, 0.0)
    expert_gate = 2.827 * chosen / jnp.sum(chosen, axis=-1, keepdims=True)
    slot_table = (placement[:, None] == expert_ids[None, :]).astype(F32)
    slot_gate = jnp.dot(expert_gate, slot_table, precision=lax.Precision.HIGHEST)
    expert_sum = experts_by_exchange(normed_half, slot_gate, up_weight, down_weight)
    return (state_half + expert_sum).astype(BF16)


def solution(mesh):
    ring = mesh.shape["ep"] == RING
    in_specs = (
        P(("replica", "ep"), None),
        P("tp", ("replica", "ep"), None),
        P(),
        P("tp", None),
        P(("replica", "ep"), None),
        P(),
        P("tp", "ep"),
        P("ep", "tp"),
    )
    out_specs = P(("replica", "ep"), "tp")
    return jax.shard_map(
        functools.partial(on_device, ring), mesh=mesh, in_specs=in_specs, out_specs=out_specs, check_vma=False
    )
```

```python
import functools

import jax
import jax.numpy as jnp
from jax import lax
from jax.experimental import pallas as pl
from jax.experimental.pallas import tpu as pltpu
from jax.sharding import PartitionSpec as P

FF_E = 1024
CAP = 12
RING = 8
UP_BUFS = 6
DOWN_BUFS = 12
PARTS = 2
MESH = pl.DeviceIdType.MESH
F32 = jnp.float32
BF16 = jnp.bfloat16


def nt_dot(a, b):
    return lax.dot_general(a, b, (((1,), (1,)), ((), ())), preferred_element_type=F32)


def dot(a, b):
    return jnp.dot(a, b, preferred_element_type=F32)


def ring_device(pos):
    back = pos // (RING // 2)
    return (1 - back) * 2 * pos + back * (2 * (RING - 1 - pos) + 1)


def expert_kernel(
    slots, res_ref, dense_ref, gain_ref, router_ref, routes_ref, place_ref, up_ref, down_ref, out_ref,
    gain_row, theirs, state, stat_own, stat_peer, d_send, d_recv, gather, xy, pre_own, pre_peer, sel, sel_t, gate_col,
    send_buf, recv_buf, up_buf, down_buf, up_sem, down_sem, g_send, g_recv, p_send, p_recv, r_send, r_recv,
):
    tok, full_width = res_ref.shape
    experts = router_ref.shape[0]
    width_ext = gather.shape[2]
    part_w = down_buf.shape[2]
    width = part_w * PARTS
    span = FF_E
    cap = CAP * RING
    total_rows = slots * cap
    tokens = tok * RING
    half = tok // 2

    ep = lax.axis_index("ep")
    tp = lax.axis_index("tp")
    x_pos = lax.rem(ep, 2)
    z_pos = ep // 2
    pos = z_pos + x_pos * (RING - 1 - 2 * z_pos)
    right = ring_device(lax.rem(pos + 1, RING))
    left = ring_device(lax.rem(pos + RING - 1, RING))
    sides = (right, left)
    step_of = (1, -1)

    def up_copy(s):
        b = lax.rem(s, UP_BUFS)
        return pltpu.make_async_copy(
            up_ref.at[:, pl.ds(pl.multiple_of(s * span, span), span)], up_buf.at[b], up_sem.at[b]
        )

    def down_copy(j):
        part = j // slots
        s = j - part * slots
        b = lax.rem(j, DOWN_BUFS)
        return pltpu.make_async_copy(
            down_ref.at[
                pl.ds(pl.multiple_of(s * span, span), span),
                pl.ds(pl.multiple_of(part * part_w, part_w), part_w),
            ],
            down_buf.at[b],
            down_sem.at[b],
        )

    barrier = pltpu.get_barrier_semaphore()
    for side in sides:
        pl.semaphore_signal(barrier, inc=1, device_id={"ep": side}, device_id_type=MESH)
    pl.semaphore_signal(barrier, inc=1, device_id={"tp": 1 - tp}, device_id_type=MESH)
    for s in range(UP_BUFS):
        up_copy(s).start()
    for j in range(DOWN_BUFS):
        down_copy(j).start()
    pl.semaphore_wait(barrier, 3)

    gain_row[...] = gain_ref[...].reshape(1, full_width)
    mine = pl.ds(pl.multiple_of(tp * width, width), width)
    other = pl.ds(pl.multiple_of((1 - tp) * width, width), width)
    dense_copy = pltpu.make_async_remote_copy(
        src_ref=dense_ref.at[0, :, other], dst_ref=theirs, send_sem=d_send.at[0], recv_sem=d_recv.at[0],
        device_id={"tp": 1 - tp}, device_id_type=MESH,
    )
    dense_copy.start()
    partial = res_ref[:, mine].astype(F32)
    own_dense = dense_ref[0, :, mine].astype(F32)
    dense_copy.wait()
    total = partial + (own_dense + theirs[...].astype(F32))
    state[...] = total
    scaled = total * gain_row[:, mine]
    stat_own[:, :experts] = lax.dot_general(
        scaled, router_ref[...].astype(F32), (((1,), (1,)), ((), ())),
        precision=lax.Precision.HIGHEST, preferred_element_type=F32,
    )
    square = jnp.sum(total * total, axis=1, keepdims=True)
    stat_own[:, experts:] = jnp.broadcast_to(square, (tok, stat_own.shape[1] - experts))
    stat_copy = pltpu.make_async_remote_copy(
        src_ref=stat_own, dst_ref=stat_peer, send_sem=d_send.at[1], recv_sem=d_recv.at[1],
        device_id={"tp": 1 - tp}, device_id_type=MESH,
    )
    stat_copy.start()
    expert_id = lax.broadcasted_iota(jnp.int32, (experts, tok), 0)
    routed_t = routes_ref[0:1, :] == expert_id
    for r in range(1, routes_ref.shape[0]):
        routed_t = routed_t | (routes_ref[r : r + 1, :] == expert_id)
    same = lax.broadcasted_iota(jnp.int32, (tok, tok), 0) == lax.broadcasted_iota(jnp.int32, (tok, tok), 1)
    routed = nt_dot(same.astype(F32).astype(BF16), routed_t.astype(F32).astype(BF16)) > 0.0
    table = place_ref[...] == lax.broadcasted_iota(jnp.int32, (experts, experts), 0)
    table = table.astype(F32).astype(BF16)
    stat_copy.wait()
    logits = stat_own[:, :experts] + stat_peer[:, :experts]
    mean_sq = (stat_own[:, experts : experts + 1] + stat_peer[:, experts : experts + 1]) / full_width
    scale = lax.rsqrt(mean_sq + 1e-06)
    gather[pos, :, :width] = (state[...] * gain_row[:, mine] * scale).astype(BF16)
    chosen = jnp.where(routed, jax.nn.sigmoid(logits * scale), 0.0)
    gate = 2.827 * chosen / jnp.sum(chosen, axis=1, keepdims=True)
    high = gate.astype(BF16)
    low = (gate - high.astype(F32)).astype(BF16)
    gather[pos, :, width : width + experts] = nt_dot(high, table).astype(BF16)
    gather[pos, :, width + experts :] = nt_dot(low, table).astype(BF16)

    def gather_copy(way, k, c):
        block = lax.rem(pos - step_of[way] * k + RING, RING)
        ref = gather.at[block, pl.ds(c * half, half), :]
        return pltpu.make_async_remote_copy(
            src_ref=ref, dst_ref=ref, send_sem=g_send.at[way, k, c], recv_sem=g_recv.at[way, k, c],
            device_id={"ep": sides[way]}, device_id_type=MESH,
        )

    steps = RING // 2
    copies = {}
    for k in range(steps):
        for c in range(PARTS):
            for way in range(2):
                part = way if c == 0 else 1 - way
                if k:
                    copies[way, k - 1, part].wait_recv()
                if k == steps - 1 and part != way:
                    continue
                copies[way, k, part] = gather_copy(way, k, part)
                copies[way, k, part].start()
    for way in range(2):
        copies[way, steps - 1, way].wait_recv()
    for copy in copies.values():
        copy.wait_send()

    gates = gather[:, :, width:].reshape(tokens, width_ext - width)
    first = ep * slots
    lane = lax.broadcasted_iota(jnp.int32, (2 * experts, 128), 0)
    slot = lax.broadcasted_iota(jnp.int32, (2 * experts, 128), 1)
    inside = slot < slots
    pick_hi = ((lane == slot + first) & inside).astype(BF16)
    pick_lo = ((lane == slot + first + experts) & inside).astype(BF16)
    gate_hi = dot(gates, pick_hi).astype(BF16)
    gate_lo = dot(gates, pick_lo).astype(BF16)
    lane_t = lax.broadcasted_iota(jnp.int32, (16, 2 * experts), 1)
    slot_t = lax.broadcasted_iota(jnp.int32, (16, 2 * experts), 0)
    pick_t = ((lane_t == slot_t + first) & (slot_t < slots)).astype(BF16)
    need_t = nt_dot(pick_t, gates) > 0.0
    need = gate_hi.astype(F32) > 0.0
    t_row = lax.broadcasted_iota(jnp.int32, (tokens, tokens), 0)
    t_col = lax.broadcasted_iota(jnp.int32, (tokens, tokens), 1)
    lower = (t_col <= t_row).astype(F32).astype(BF16)
    upper = (t_row <= t_col).astype(F32).astype(BF16)
    order = dot(lower, need.astype(F32).astype(BF16))
    order_t = dot(need_t.astype(F32).astype(BF16), upper)
    order = jnp.where(need, order, 0.0).astype(BF16)
    order_t = jnp.where(need_t, order_t, 0.0).astype(BF16)

    def place_of(shape, dim):
        j = lax.broadcasted_iota(jnp.int32, shape, dim)
        c = j
        for s in range(1, slots):
            c = c - jnp.where(j >= s * cap, cap, 0)
        return (c + 1).astype(F32)

    def spread(shape, dim):
        j = lax.broadcasted_iota(jnp.int32, shape, dim)
        s = lax.broadcasted_iota(jnp.int32, shape, 1 - dim)
        return (j >= s * cap) & (j < (s + 1) * cap)

    spread_c = spread((128, total_rows), 1).astype(F32).astype(BF16)
    spread_r = spread((total_rows, 16), 0).astype(F32).astype(BF16)
    sel_t[...] = (dot(order, spread_c) == place_of((1, total_rows), 1)).astype(F32).astype(BF16)
    sel[...] = (dot(spread_r, order_t) == place_of((total_rows, 1), 0)).astype(F32).astype(BF16)
    row_gates = dot(sel[...], gate_hi) + dot(sel[...], gate_lo)
    own_slot = spread((total_rows, 128), 0)
    gate_col[...] = jnp.sum(jnp.where(own_slot, row_gates, 0.0), axis=1, keepdims=True)

    def peer_copy(s):
        return pltpu.make_async_remote_copy(
            src_ref=pre_own.at[s], dst_ref=pre_peer.at[s], send_sem=p_send.at[s], recv_sem=p_recv.at[s],
            device_id={"tp": 1 - tp}, device_id_type=MESH,
        )

    def pick_step(i, carry):
        cols = pl.ds(pl.multiple_of(i * 256, 256), 256)
        xy[:, cols] = dot(sel[...], gather[:, :, cols].reshape(tokens, 256)).astype(BF16)
        return carry

    lax.fori_loop(0, width // 256, pick_step, 0)

    def up_step(s, carry):
        at = pl.ds(pl.multiple_of(s * cap, cap), cap)
        up_copy(s).wait()
        pre_own[s] = dot(xy[at, :], up_buf[lax.rem(s, UP_BUFS)]).astype(BF16)
        peer_copy(s).start()

        @pl.when(s + UP_BUFS < slots)
        def _():
            up_copy(s + UP_BUFS).start()

        return carry

    lax.fori_loop(0, slots, up_step, 0)

    def down_step(part, s, carry):
        at = pl.ds(pl.multiple_of(s * cap, cap), cap)
        j = part * slots + s
        if part == 0:
            peer_copy(s).wait()
            pre = pre_own[s].astype(F32) + pre_peer[s].astype(F32)
            gated = (jax.nn.silu(pre) * gate_col[at, :]).astype(BF16)
            pre_own[s] = gated
        else:
            gated = pre_own[s]
        down_copy(j).wait()
        cols = slice(part * part_w, (part + 1) * part_w)
        xy[at, cols] = dot(gated, down_buf[lax.rem(j, DOWN_BUFS)]).astype(BF16)

        @pl.when(j + DOWN_BUFS < PARTS * slots)
        def _():
            down_copy(j + DOWN_BUFS).start()

        return carry

    def chunk(dest, start, rows, part):
        at = pl.ds(pl.multiple_of(dest * tok + start, half), rows)
        return dot(sel_t[at, :], xy[:, part * part_w : (part + 1) * part_w])

    def reduce_copy(way, k, part):
        at = pl.ds(way * half, half) if k == 0 else pl.ds(0, tok)
        cols = pl.ds(part * part_w, part_w)
        return pltpu.make_async_remote_copy(
            src_ref=send_buf.at[way, k, at, cols], dst_ref=recv_buf.at[way, k, at, cols],
            send_sem=r_send.at[way, k, part], recv_sem=r_recv.at[way, k, part],
            device_id={"ep": sides[way]}, device_id_type=MESH,
        )

    for part in range(PARTS):
        lax.fori_loop(0, slots, functools.partial(down_step, part), 0)
        dest = lax.rem(pos + steps, RING)
        cols = slice(part * part_w, (part + 1) * part_w)
        for way in range(2):
            rows = slice(way * half, (way + 1) * half)
            send_buf[way, 0, rows, cols] = chunk(dest, way * half, half, part).astype(BF16)
            reduce_copy(way, 0, part).start()

    for k in range(1, steps):
        for part in range(PARTS):
            cols = slice(part * part_w, (part + 1) * part_w)
            for way in range(2):
                dest = lax.rem(pos + step_of[way] * (steps - k) + RING, RING)
                own = chunk(dest, 0, tok, part)
                reduce_copy(way, k - 1, part).wait_recv()
                if k == 1:
                    at = slice(way * half, (way + 1) * half)
                    other = slice((1 - way) * half, (2 - way) * half)
                    send_buf[way, k, other, cols] = own[other].astype(BF16)
                    send_buf[way, k, at, cols] = (own[at] + recv_buf[way, 0, at, cols].astype(F32)).astype(BF16)
                else:
                    send_buf[way, k, :, cols] = (own + recv_buf[way, k - 1, :, cols].astype(F32)).astype(BF16)
                reduce_copy(way, k, part).start()
    for part in range(PARTS):
        cols = slice(part * part_w, (part + 1) * part_w)
        own = chunk(pos, 0, tok, part)
        for way in range(2):
            reduce_copy(way, steps - 1, part).wait_recv()
            own = own + recv_buf[way, steps - 1, :, cols].astype(F32)
        out_ref[:, cols] = (own + state[:, cols]).astype(out_ref.dtype)
    for way in range(2):
        for k in range(steps):
            for part in range(PARTS):
                reduce_copy(way, k, part).wait_send()


def block_on_ring(
    residual_in, dense_terms, norm_gain, router_weight, routes, placement, up_weight, down_weight
):
    tok = residual_in.shape[0]
    width = up_weight.shape[0]
    experts = placement.shape[0]
    width_ext = width + 2 * experts
    slots = up_weight.shape[1] // FF_E
    cap = CAP * RING
    steps = RING // 2
    vmem = pl.BlockSpec(memory_space=pltpu.VMEM)
    hbm = pl.BlockSpec(memory_space=pl.ANY)
    dma = pltpu.SemaphoreType.DMA
    return pl.pallas_call(
        functools.partial(expert_kernel, slots),
        out_shape=jax.ShapeDtypeStruct((tok, width), BF16),
        in_specs=[vmem] * 6 + [hbm, hbm],
        out_specs=vmem,
        scratch_shapes=[
            pltpu.VMEM((1, residual_in.shape[1]), F32),
            pltpu.VMEM((tok, width), BF16),
            pltpu.VMEM((tok, width), F32),
            pltpu.VMEM((tok, 2 * experts), F32),
            pltpu.VMEM((tok, 2 * experts), F32),
            dma((2,)),
            dma((2,)),
            pltpu.VMEM((RING, tok, width_ext), BF16),
            pltpu.VMEM((slots * cap, width), BF16),
            pltpu.VMEM((slots, cap, FF_E), BF16),
            pltpu.VMEM((slots, cap, FF_E), BF16),
            pltpu.VMEM((slots * cap, RING * tok), BF16),
            pltpu.VMEM((RING * tok, slots * cap), BF16),
            pltpu.VMEM((slots * cap, 1), F32),
            pltpu.VMEM((2, steps, tok, width), BF16),
            pltpu.VMEM((2, steps, tok, width), BF16),
            pltpu.VMEM((UP_BUFS, width, FF_E), BF16),
            pltpu.VMEM((DOWN_BUFS, FF_E, width // PARTS), BF16),
            dma((UP_BUFS,)),
            dma((DOWN_BUFS,)),
            dma((2, steps, PARTS)),
            dma((2, steps, PARTS)),
            dma((slots,)),
            dma((slots,)),
            dma((2, steps, PARTS)),
            dma((2, steps, PARTS)),
        ],
        compiler_params=pltpu.CompilerParams(
            collective_id=0, has_side_effects=True, vmem_limit_bytes=62 * 1024 * 1024
        ),
    )(
        residual_in, dense_terms, norm_gain, router_weight.T, routes.T, placement[None], up_weight, down_weight
    )


def experts_by_exchange(normed_half, slot_gate, up_weight, down_weight):
    columns = up_weight.shape[1]
    tok_rows = normed_half.shape[0]
    experts = slot_gate.shape[1]
    peers = lax.axis_size("ep")
    local_slots = max(1, columns // FF_E)
    span = min(FF_E, columns)
    capacity = min(tok_rows, CAP * local_slots)
    expert_ids = jnp.arange(experts, dtype=jnp.int32)
    peer_ids = jnp.arange(peers, dtype=jnp.int32)
    slot_of_peer = (
        peer_ids[:, None] * columns // FF_E + jnp.arange(local_slots, dtype=jnp.int32)[None, :]
    )
    pick_table = (slot_of_peer[:, :, None] == expert_ids[None, None, :]).astype(F32)
    peer_gates = jnp.einsum("ts,pls->tpl", slot_gate, pick_table, precision=lax.Precision.HIGHEST)
    need = (jnp.sum(peer_gates, axis=-1) > 0.0).astype(jnp.int32)
    position = jnp.cumsum(need, axis=0) - 1
    slot_pos = jnp.arange(capacity, dtype=jnp.int32)
    selector = (need.T[:, None, :] == 1) & (position.T[:, None, :] == slot_pos[None, :, None])
    select_b = selector.astype(BF16)
    send_gates = jnp.einsum(
        "pct,tpl->pcl", selector.astype(F32), peer_gates, precision=lax.Precision.HIGHEST
    )
    send_rows = jnp.einsum(
        "pct,tf->pcf", select_b, normed_half.astype(BF16), preferred_element_type=F32
    ).astype(BF16)
    rows_in = lax.all_to_all(send_rows, "ep", split_axis=0, concat_axis=0, tiled=True)
    gates_in = lax.all_to_all(
        send_gates.astype(BF16), "ep", split_axis=0, concat_axis=0, tiled=True
    ).astype(F32)
    part_pre = jnp.einsum("sif,fh->sih", rows_in, up_weight, preferred_element_type=F32)
    pre = lax.psum(part_pre.astype(BF16), "tp").astype(F32)
    column_gate = jnp.repeat(gates_in, span, axis=2)
    gated = (jax.nn.silu(pre) * column_gate).astype(BF16)
    result = jnp.einsum("sih,hf->sif", gated, down_weight, preferred_element_type=F32).astype(BF16)
    returned = lax.all_to_all(result, "ep", split_axis=0, concat_axis=0, tiled=True)
    return jnp.einsum("pct,pcf->tf", select_b, returned, preferred_element_type=F32)


def on_device(
    ring, residual_in, dense_terms, norm_gain, router_weight, routes, placement, up_weight, down_weight
):
    if ring:
        return block_on_ring(
            residual_in, dense_terms, norm_gain, router_weight, routes, placement, up_weight, down_weight
        )
    half_width = up_weight.shape[0]
    experts = placement.shape[0]
    full_width = residual_in.shape[1]
    tp = lax.axis_index("tp")
    start = tp * half_width
    other = (1 - tp) * half_width

    def cut(a, at):
        return lax.dynamic_slice_in_dim(a, at, half_width, a.ndim - 1)

    theirs = lax.ppermute(cut(dense_terms[0], other), "tp", [(0, 1), (1, 0)])
    state_half = cut(residual_in, start).astype(F32) + (
        cut(dense_terms[0], start).astype(F32) + theirs.astype(F32)
    )
    scaled = state_half * cut(norm_gain, start)
    part_logits = jnp.dot(scaled, router_weight.astype(F32), precision=lax.Precision.HIGHEST)
    part_sq = jnp.sum(state_half * state_half, axis=-1, keepdims=True)
    sums = lax.psum(jnp.concatenate([part_logits, part_sq], axis=1), "tp")
    scale = lax.rsqrt(sums[:, experts:] / full_width + 1e-06)
    scores = jax.nn.sigmoid(sums[:, :experts] * scale)
    normed_half = scaled * scale
    expert_ids = jnp.arange(experts, dtype=jnp.int32)
    routed = jnp.any(routes[:, :, None] == expert_ids[None, None, :], axis=1)
    chosen = jnp.where(routed, scores, 0.0)
    expert_gate = 2.827 * chosen / jnp.sum(chosen, axis=-1, keepdims=True)
    slot_table = (placement[:, None] == expert_ids[None, :]).astype(F32)
    slot_gate = jnp.dot(expert_gate, slot_table, precision=lax.Precision.HIGHEST)
    expert_sum = experts_by_exchange(normed_half, slot_gate, up_weight, down_weight)
    return (state_half + expert_sum).astype(BF16)


def solution(mesh):
    ring = mesh.shape["ep"] == RING
    in_specs = (
        P(("replica", "ep"), None),
        P("tp", ("replica", "ep"), None),
        P(),
        P("tp", None),
        P(("replica", "ep"), None),
        P(),
        P("tp", "ep"),
        P("ep", "tp"),
    )
    out_specs = P(("replica", "ep"), "tp")
    return jax.shard_map(
        functools.partial(on_device, ring), mesh=mesh, in_specs=in_specs, out_specs=out_specs, check_vma=False
    )
```

```python
import functools

import jax
import jax.numpy as jnp
from jax import lax
from jax.experimental import pallas as pl
from jax.experimental.pallas import tpu as pltpu
from jax.sharding import PartitionSpec as P

FF_E = 1024
CAP = 12
RING = 8
UP_BUFS = 6
DOWN_BUFS = 12
PARTS = 2
ROW_PARTS = 4
MESH = pl.DeviceIdType.MESH
F32 = jnp.float32
BF16 = jnp.bfloat16


def nt_dot(a, b):
    return lax.dot_general(a, b, (((1,), (1,)), ((), ())), preferred_element_type=F32)


def dot(a, b):
    return jnp.dot(a, b, preferred_element_type=F32)


def ring_device(pos):
    back = pos // (RING // 2)
    return (1 - back) * 2 * pos + back * (2 * (RING - 1 - pos) + 1)


def expert_kernel(
    slots, res_ref, dense_ref, gain_ref, router_ref, routes_ref, place_ref, up_ref, down_ref, out_ref,
    gain_row, theirs, state, stat_own, stat_peer, d_send, d_recv, gather, xy, pre_own, pre_peer, sel, sel_t, gate_col,
    send_buf, recv_buf, up_buf, down_buf, up_sem, down_sem, g_send, g_recv, p_send, p_recv, r_send, r_recv,
):
    tok, full_width = res_ref.shape
    experts = router_ref.shape[0]
    width_ext = gather.shape[2]
    part_w = down_buf.shape[2]
    width = part_w * PARTS
    span = FF_E
    cap = CAP * RING
    total_rows = slots * cap
    tokens = tok * RING
    half = tok // 2
    piece = tok // ROW_PARTS

    ep = lax.axis_index("ep")
    tp = lax.axis_index("tp")
    x_pos = lax.rem(ep, 2)
    z_pos = ep // 2
    pos = z_pos + x_pos * (RING - 1 - 2 * z_pos)
    right = ring_device(lax.rem(pos + 1, RING))
    left = ring_device(lax.rem(pos + RING - 1, RING))
    sides = (right, left)
    step_of = (1, -1)

    def up_copy(s):
        b = lax.rem(s, UP_BUFS)
        return pltpu.make_async_copy(
            up_ref.at[:, pl.ds(pl.multiple_of(s * span, span), span)], up_buf.at[b], up_sem.at[b]
        )

    def down_copy(j):
        part = j // slots
        s = j - part * slots
        b = lax.rem(j, DOWN_BUFS)
        return pltpu.make_async_copy(
            down_ref.at[
                pl.ds(pl.multiple_of(s * span, span), span),
                pl.ds(pl.multiple_of(part * part_w, part_w), part_w),
            ],
            down_buf.at[b],
            down_sem.at[b],
        )

    barrier = pltpu.get_barrier_semaphore()
    for side in sides:
        pl.semaphore_signal(barrier, inc=1, device_id={"ep": side}, device_id_type=MESH)
    pl.semaphore_signal(barrier, inc=1, device_id={"tp": 1 - tp}, device_id_type=MESH)
    for s in range(UP_BUFS):
        up_copy(s).start()
    for j in range(DOWN_BUFS):
        down_copy(j).start()
    pl.semaphore_wait(barrier, 3)

    gain_row[...] = gain_ref[...].reshape(1, full_width)
    mine = pl.ds(pl.multiple_of(tp * width, width), width)
    other = pl.ds(pl.multiple_of((1 - tp) * width, width), width)
    dense_copy = pltpu.make_async_remote_copy(
        src_ref=dense_ref.at[0, :, other], dst_ref=theirs, send_sem=d_send.at[0], recv_sem=d_recv.at[0],
        device_id={"tp": 1 - tp}, device_id_type=MESH,
    )
    dense_copy.start()
    partial = res_ref[:, mine].astype(F32)
    own_dense = dense_ref[0, :, mine].astype(F32)
    dense_copy.wait()
    total = partial + (own_dense + theirs[...].astype(F32))
    state[...] = total
    scaled = total * gain_row[:, mine]
    stat_own[:, :experts] = lax.dot_general(
        scaled, router_ref[...].astype(F32), (((1,), (1,)), ((), ())),
        precision=lax.Precision.HIGHEST, preferred_element_type=F32,
    )
    square = jnp.sum(total * total, axis=1, keepdims=True)
    stat_own[:, experts:] = jnp.broadcast_to(square, (tok, stat_own.shape[1] - experts))
    stat_copy = pltpu.make_async_remote_copy(
        src_ref=stat_own, dst_ref=stat_peer, send_sem=d_send.at[1], recv_sem=d_recv.at[1],
        device_id={"tp": 1 - tp}, device_id_type=MESH,
    )
    stat_copy.start()
    expert_id = lax.broadcasted_iota(jnp.int32, (experts, tok), 0)
    routed_t = routes_ref[0:1, :] == expert_id
    for r in range(1, routes_ref.shape[0]):
        routed_t = routed_t | (routes_ref[r : r + 1, :] == expert_id)
    same = lax.broadcasted_iota(jnp.int32, (tok, tok), 0) == lax.broadcasted_iota(jnp.int32, (tok, tok), 1)
    routed = nt_dot(same.astype(F32).astype(BF16), routed_t.astype(F32).astype(BF16)) > 0.0
    table = place_ref[...] == lax.broadcasted_iota(jnp.int32, (experts, experts), 0)
    table = table.astype(F32).astype(BF16)
    stat_copy.wait()
    logits = stat_own[:, :experts] + stat_peer[:, :experts]
    mean_sq = (stat_own[:, experts : experts + 1] + stat_peer[:, experts : experts + 1]) / full_width
    scale = lax.rsqrt(mean_sq + 1e-06)
    gather[pos, :, :width] = (state[...] * gain_row[:, mine] * scale).astype(BF16)
    chosen = jnp.where(routed, jax.nn.sigmoid(logits * scale), 0.0)
    gate = 2.827 * chosen / jnp.sum(chosen, axis=1, keepdims=True)
    high = gate.astype(BF16)
    low = (gate - high.astype(F32)).astype(BF16)
    gather[pos, :, width : width + experts] = nt_dot(high, table).astype(BF16)
    gather[pos, :, width + experts :] = nt_dot(low, table).astype(BF16)

    def gather_copy(way, k, c):
        block = lax.rem(pos - step_of[way] * k + RING, RING)
        ref = gather.at[block, pl.ds(c * piece, piece), :]
        return pltpu.make_async_remote_copy(
            src_ref=ref, dst_ref=ref, send_sem=g_send.at[way, k, c], recv_sem=g_recv.at[way, k, c],
            device_id={"ep": sides[way]}, device_id_type=MESH,
        )

    steps = RING // 2
    copies = {}
    for k in range(steps):
        for c in range(ROW_PARTS):
            for way in range(2):
                part = (c + way * (ROW_PARTS // 2)) % ROW_PARTS
                if k:
                    copies[way, k - 1, part].wait_recv()
                if k == steps - 1 and c >= ROW_PARTS // 2:
                    continue
                copies[way, k, part] = gather_copy(way, k, part)
                copies[way, k, part].start()
    for way in range(2):
        for c in range(ROW_PARTS // 2):
            copies[way, steps - 1, c + way * (ROW_PARTS // 2)].wait_recv()
    for copy in copies.values():
        copy.wait_send()

    gates = gather[:, :, width:].reshape(tokens, width_ext - width)
    first = ep * slots
    lane = lax.broadcasted_iota(jnp.int32, (2 * experts, 128), 0)
    slot = lax.broadcasted_iota(jnp.int32, (2 * experts, 128), 1)
    inside = slot < slots
    pick_hi = ((lane == slot + first) & inside).astype(BF16)
    pick_lo = ((lane == slot + first + experts) & inside).astype(BF16)
    gate_hi = dot(gates, pick_hi).astype(BF16)
    gate_lo = dot(gates, pick_lo).astype(BF16)
    lane_t = lax.broadcasted_iota(jnp.int32, (16, 2 * experts), 1)
    slot_t = lax.broadcasted_iota(jnp.int32, (16, 2 * experts), 0)
    pick_t = ((lane_t == slot_t + first) & (slot_t < slots)).astype(BF16)
    need_t = nt_dot(pick_t, gates) > 0.0
    need = gate_hi.astype(F32) > 0.0
    t_row = lax.broadcasted_iota(jnp.int32, (tokens, tokens), 0)
    t_col = lax.broadcasted_iota(jnp.int32, (tokens, tokens), 1)
    lower = (t_col <= t_row).astype(F32).astype(BF16)
    upper = (t_row <= t_col).astype(F32).astype(BF16)
    order = dot(lower, need.astype(F32).astype(BF16))
    order_t = dot(need_t.astype(F32).astype(BF16), upper)
    order = jnp.where(need, order, 0.0).astype(BF16)
    order_t = jnp.where(need_t, order_t, 0.0).astype(BF16)

    def place_of(shape, dim):
        j = lax.broadcasted_iota(jnp.int32, shape, dim)
        c = j
        for s in range(1, slots):
            c = c - jnp.where(j >= s * cap, cap, 0)
        return (c + 1).astype(F32)

    def spread(shape, dim):
        j = lax.broadcasted_iota(jnp.int32, shape, dim)
        s = lax.broadcasted_iota(jnp.int32, shape, 1 - dim)
        return (j >= s * cap) & (j < (s + 1) * cap)

    spread_c = spread((128, total_rows), 1).astype(F32).astype(BF16)
    spread_r = spread((total_rows, 16), 0).astype(F32).astype(BF16)
    sel_t[...] = (dot(order, spread_c) == place_of((1, total_rows), 1)).astype(F32).astype(BF16)
    sel[...] = (dot(spread_r, order_t) == place_of((total_rows, 1), 0)).astype(F32).astype(BF16)
    row_gates = dot(sel[...], gate_hi) + dot(sel[...], gate_lo)
    own_slot = spread((total_rows, 128), 0)
    gate_col[...] = jnp.sum(jnp.where(own_slot, row_gates, 0.0), axis=1, keepdims=True)

    def peer_copy(s):
        return pltpu.make_async_remote_copy(
            src_ref=pre_own.at[s], dst_ref=pre_peer.at[s], send_sem=p_send.at[s], recv_sem=p_recv.at[s],
            device_id={"tp": 1 - tp}, device_id_type=MESH,
        )

    def pick_step(i, carry):
        cols = pl.ds(pl.multiple_of(i * 256, 256), 256)
        xy[:, cols] = dot(sel[...], gather[:, :, cols].reshape(tokens, 256)).astype(BF16)
        return carry

    lax.fori_loop(0, width // 256, pick_step, 0)

    def up_step(s, carry):
        at = pl.ds(pl.multiple_of(s * cap, cap), cap)
        up_copy(s).wait()
        pre_own[s] = dot(xy[at, :], up_buf[lax.rem(s, UP_BUFS)]).astype(BF16)
        peer_copy(s).start()

        @pl.when(s + UP_BUFS < slots)
        def _():
            up_copy(s + UP_BUFS).start()

        return carry

    lax.fori_loop(0, slots, up_step, 0)

    def down_step(part, s, carry):
        at = pl.ds(pl.multiple_of(s * cap, cap), cap)
        j = part * slots + s
        if part == 0:
            peer_copy(s).wait()
            pre = pre_own[s].astype(F32) + pre_peer[s].astype(F32)
            gated = (jax.nn.silu(pre) * gate_col[at, :]).astype(BF16)
            pre_own[s] = gated
        else:
            gated = pre_own[s]
        down_copy(j).wait()
        cols = slice(part * part_w, (part + 1) * part_w)
        xy[at, cols] = dot(gated, down_buf[lax.rem(j, DOWN_BUFS)]).astype(BF16)

        @pl.when(j + DOWN_BUFS < PARTS * slots)
        def _():
            down_copy(j + DOWN_BUFS).start()

        return carry

    def chunk(dest, start, rows, part):
        at = pl.ds(pl.multiple_of(dest * tok + start, half), rows)
        return dot(sel_t[at, :], xy[:, part * part_w : (part + 1) * part_w])

    def reduce_copy(way, k, part):
        at = pl.ds(way * half, half) if k == 0 else pl.ds(0, tok)
        cols = pl.ds(part * part_w, part_w)
        return pltpu.make_async_remote_copy(
            src_ref=send_buf.at[way, k, at, cols], dst_ref=recv_buf.at[way, k, at, cols],
            send_sem=r_send.at[way, k, part], recv_sem=r_recv.at[way, k, part],
            device_id={"ep": sides[way]}, device_id_type=MESH,
        )

    for part in range(PARTS):
        lax.fori_loop(0, slots, functools.partial(down_step, part), 0)
        dest = lax.rem(pos + steps, RING)
        cols = slice(part * part_w, (part + 1) * part_w)
        for way in range(2):
            rows = slice(way * half, (way + 1) * half)
            send_buf[way, 0, rows, cols] = chunk(dest, way * half, half, part).astype(BF16)
            reduce_copy(way, 0, part).start()

    for k in range(1, steps):
        for part in range(PARTS):
            cols = slice(part * part_w, (part + 1) * part_w)
            for way in range(2):
                dest = lax.rem(pos + step_of[way] * (steps - k) + RING, RING)
                own = chunk(dest, 0, tok, part)
                reduce_copy(way, k - 1, part).wait_recv()
                if k == 1:
                    at = slice(way * half, (way + 1) * half)
                    other = slice((1 - way) * half, (2 - way) * half)
                    send_buf[way, k, other, cols] = own[other].astype(BF16)
                    send_buf[way, k, at, cols] = (own[at] + recv_buf[way, 0, at, cols].astype(F32)).astype(BF16)
                else:
                    send_buf[way, k, :, cols] = (own + recv_buf[way, k - 1, :, cols].astype(F32)).astype(BF16)
                reduce_copy(way, k, part).start()
    for part in range(PARTS):
        cols = slice(part * part_w, (part + 1) * part_w)
        own = chunk(pos, 0, tok, part)
        for way in range(2):
            reduce_copy(way, steps - 1, part).wait_recv()
            own = own + recv_buf[way, steps - 1, :, cols].astype(F32)
        out_ref[:, cols] = (own + state[:, cols]).astype(out_ref.dtype)
    for way in range(2):
        for k in range(steps):
            for part in range(PARTS):
                reduce_copy(way, k, part).wait_send()


def block_on_ring(
    residual_in, dense_terms, norm_gain, router_weight, routes, placement, up_weight, down_weight
):
    tok = residual_in.shape[0]
    width = up_weight.shape[0]
    experts = placement.shape[0]
    width_ext = width + 2 * experts
    slots = up_weight.shape[1] // FF_E
    cap = CAP * RING
    steps = RING // 2
    vmem = pl.BlockSpec(memory_space=pltpu.VMEM)
    hbm = pl.BlockSpec(memory_space=pl.ANY)
    dma = pltpu.SemaphoreType.DMA
    return pl.pallas_call(
        functools.partial(expert_kernel, slots),
        out_shape=jax.ShapeDtypeStruct((tok, width), BF16),
        in_specs=[vmem] * 6 + [hbm, hbm],
        out_specs=vmem,
        scratch_shapes=[
            pltpu.VMEM((1, residual_in.shape[1]), F32),
            pltpu.VMEM((tok, width), BF16),
            pltpu.VMEM((tok, width), F32),
            pltpu.VMEM((tok, 2 * experts), F32),
            pltpu.VMEM((tok, 2 * experts), F32),
            dma((2,)),
            dma((2,)),
            pltpu.VMEM((RING, tok, width_ext), BF16),
            pltpu.VMEM((slots * cap, width), BF16),
            pltpu.VMEM((slots, cap, FF_E), BF16),
            pltpu.VMEM((slots, cap, FF_E), BF16),
            pltpu.VMEM((slots * cap, RING * tok), BF16),
            pltpu.VMEM((RING * tok, slots * cap), BF16),
            pltpu.VMEM((slots * cap, 1), F32),
            pltpu.VMEM((2, steps, tok, width), BF16),
            pltpu.VMEM((2, steps, tok, width), BF16),
            pltpu.VMEM((UP_BUFS, width, FF_E), BF16),
            pltpu.VMEM((DOWN_BUFS, FF_E, width // PARTS), BF16),
            dma((UP_BUFS,)),
            dma((DOWN_BUFS,)),
            dma((2, steps, ROW_PARTS)),
            dma((2, steps, ROW_PARTS)),
            dma((slots,)),
            dma((slots,)),
            dma((2, steps, PARTS)),
            dma((2, steps, PARTS)),
        ],
        compiler_params=pltpu.CompilerParams(
            collective_id=0, has_side_effects=True, vmem_limit_bytes=62 * 1024 * 1024
        ),
    )(
        residual_in, dense_terms, norm_gain, router_weight.T, routes.T, placement[None], up_weight, down_weight
    )


def experts_by_exchange(normed_half, slot_gate, up_weight, down_weight):
    columns = up_weight.shape[1]
    tok_rows = normed_half.shape[0]
    experts = slot_gate.shape[1]
    peers = lax.axis_size("ep")
    local_slots = max(1, columns // FF_E)
    span = min(FF_E, columns)
    capacity = min(tok_rows, CAP * local_slots)
    expert_ids = jnp.arange(experts, dtype=jnp.int32)
    peer_ids = jnp.arange(peers, dtype=jnp.int32)
    slot_of_peer = (
        peer_ids[:, None] * columns // FF_E + jnp.arange(local_slots, dtype=jnp.int32)[None, :]
    )
    pick_table = (slot_of_peer[:, :, None] == expert_ids[None, None, :]).astype(F32)
    peer_gates = jnp.einsum("ts,pls->tpl", slot_gate, pick_table, precision=lax.Precision.HIGHEST)
    need = (jnp.sum(peer_gates, axis=-1) > 0.0).astype(jnp.int32)
    position = jnp.cumsum(need, axis=0) - 1
    slot_pos = jnp.arange(capacity, dtype=jnp.int32)
    selector = (need.T[:, None, :] == 1) & (position.T[:, None, :] == slot_pos[None, :, None])
    select_b = selector.astype(BF16)
    send_gates = jnp.einsum(
        "pct,tpl->pcl", selector.astype(F32), peer_gates, precision=lax.Precision.HIGHEST
    )
    send_rows = jnp.einsum(
        "pct,tf->pcf", select_b, normed_half.astype(BF16), preferred_element_type=F32
    ).astype(BF16)
    rows_in = lax.all_to_all(send_rows, "ep", split_axis=0, concat_axis=0, tiled=True)
    gates_in = lax.all_to_all(
        send_gates.astype(BF16), "ep", split_axis=0, concat_axis=0, tiled=True
    ).astype(F32)
    part_pre = jnp.einsum("sif,fh->sih", rows_in, up_weight, preferred_element_type=F32)
    pre = lax.psum(part_pre.astype(BF16), "tp").astype(F32)
    column_gate = jnp.repeat(gates_in, span, axis=2)
    gated = (jax.nn.silu(pre) * column_gate).astype(BF16)
    result = jnp.einsum("sih,hf->sif", gated, down_weight, preferred_element_type=F32).astype(BF16)
    returned = lax.all_to_all(result, "ep", split_axis=0, concat_axis=0, tiled=True)
    return jnp.einsum("pct,pcf->tf", select_b, returned, preferred_element_type=F32)


def on_device(
    ring, residual_in, dense_terms, norm_gain, router_weight, routes, placement, up_weight, down_weight
):
    if ring:
        return block_on_ring(
            residual_in, dense_terms, norm_gain, router_weight, routes, placement, up_weight, down_weight
        )
    half_width = up_weight.shape[0]
    experts = placement.shape[0]
    full_width = residual_in.shape[1]
    tp = lax.axis_index("tp")
    start = tp * half_width
    other = (1 - tp) * half_width

    def cut(a, at):
        return lax.dynamic_slice_in_dim(a, at, half_width, a.ndim - 1)

    theirs = lax.ppermute(cut(dense_terms[0], other), "tp", [(0, 1), (1, 0)])
    state_half = cut(residual_in, start).astype(F32) + (
        cut(dense_terms[0], start).astype(F32) + theirs.astype(F32)
    )
    scaled = state_half * cut(norm_gain, start)
    part_logits = jnp.dot(scaled, router_weight.astype(F32), precision=lax.Precision.HIGHEST)
    part_sq = jnp.sum(state_half * state_half, axis=-1, keepdims=True)
    sums = lax.psum(jnp.concatenate([part_logits, part_sq], axis=1), "tp")
    scale = lax.rsqrt(sums[:, experts:] / full_width + 1e-06)
    scores = jax.nn.sigmoid(sums[:, :experts] * scale)
    normed_half = scaled * scale
    expert_ids = jnp.arange(experts, dtype=jnp.int32)
    routed = jnp.any(routes[:, :, None] == expert_ids[None, None, :], axis=1)
    chosen = jnp.where(routed, scores, 0.0)
    expert_gate = 2.827 * chosen / jnp.sum(chosen, axis=-1, keepdims=True)
    slot_table = (placement[:, None] == expert_ids[None, :]).astype(F32)
    slot_gate = jnp.dot(expert_gate, slot_table, precision=lax.Precision.HIGHEST)
    expert_sum = experts_by_exchange(normed_half, slot_gate, up_weight, down_weight)
    return (state_half + expert_sum).astype(BF16)


def solution(mesh):
    ring = mesh.shape["ep"] == RING
    in_specs = (
        P(("replica", "ep"), None),
        P("tp", ("replica", "ep"), None),
        P(),
        P("tp", None),
        P(("replica", "ep"), None),
        P(),
        P("tp", "ep"),
        P("ep", "tp"),
    )
    out_specs = P(("replica", "ep"), "tp")
    return jax.shard_map(
        functools.partial(on_device, ring), mesh=mesh, in_specs=in_specs, out_specs=out_specs, check_vma=False
    )
```
